256 devices in a mesh: section: 16 (over z, x_hi), blk: 16 (over x_lo, y, core).
Axes of the slice: x: 4 (x_hi: 2, x_lo: 2; x = x_hi * 2 + x_lo), y: 4, z: 8, core: 2. Of those that a mesh axis runs over, the one named last changes fastest.
Arguments:
- states: bfloat16 [16, 2048, 1216], P('section', 'blk'), may hold values from -6 to 6
- image_weight: bfloat16 [16, 1216, 3648], P('section'), may hold values from -0.15625 to 0.15625
- text_weight: bfloat16 [16, 1216, 2432], P('section', None, 'blk'), may hold values from -0.15625 to 0.15625
- text_states: bfloat16 [16, 256, 1216], P('section'), may hold values from -6 to 6
- stale_cache: bfloat16 [16, 2, 2048, 2432], P('section', None, 'blk'), may hold values from -3 to 3
- modulation: float32 [28, 16, 5, 1216], P(None, 'section'), may hold values from -4 to 4
- query_gain: float32 [16, 64], P('section'), may hold values from 0.5 to 3
- key_gain: float32 [16, 64], P('section'), may hold values from 0.5 to 3
- text_gain: float32 [16, 64], P('section'), may hold values from 0.5 to 3
- timestep: int32 [16], P('section'), may hold values from 0 to 27
- layer_patch_index: int32 [16], P('section'), may hold values from 0 to 1
Outputs:
- next_states: bfloat16 [16, 2048, 1216], P('section', 'blk')
- fresh_entries: bfloat16 [16, 2048, 2432], P('section', 'blk')
The draws below stay inside these ranges and needn't reach their ends.
Inputs may be any that keep to these rules, and one draw needn't show every extreme that they name: `timestep`: index of a row of the modulation table. `layer_patch_index`: a patch number.
All inputs are finite; a program needn't handle non-finite values.
Results may differ from the reference program's by a relative error of at most 0.0055.
Values may be sent and summed in bfloat16 or wider, within the bound.
A program may use at most 192 MiB of HBM per device.

```python
import math
import jax
import jax.numpy as jnp
from jax import lax

PATCHES = 2
HEADS = 19
HDIM = 64
TEXT = 256
STEPS = 28
D = 1216
LAYERS = 16
PATCH_TOK = 2048


def plant(values, stream_key, smallest, high):
    index_at = [jax.random.randint(jax.random.fold_in(stream_key, axis), (), 0, length) for axis, length in enumerate(values.shape)]
    main_axis = values.shape.index(max(values.shape))
    beside = index_at[:main_axis] + [(index_at[main_axis] + 1) % values.shape[main_axis]] + index_at[main_axis + 1:]
    return values.at[tuple(index_at)].set(smallest).at[tuple(beside)].set(high)


def level_of(rng, extent, cuts, low, top_value):
    factor_of, own = 1.0, jax.random.fold_in(rng, 6)
    for position, parts in cuts:
        draws = jnp.exp(jax.random.uniform(jax.random.fold_in(own, position), (parts,), jnp.float32, low / len(cuts), top_value / len(cuts)))
        factor_of = factor_of * jnp.repeat(draws, extent[position] // parts).reshape([-1 if axis == position else 1 for axis in range(len(extent))])
    return factor_of


def bell_draw(key, shape, deviation, reach, shards=(), kind=jnp.bfloat16):
    gain = level_of(key, shape, shards, -0.22, 0.18) if shards else 1.0
    array = jax.random.normal(key, shape, jnp.float32) * deviation * gain
    return jnp.minimum(jnp.maximum(array, -reach), reach).astype(kind)


def setup_inputs(seed: int = 0) -> dict:
    key_of = jax.random.split(jax.random.key(seed), 12)
    states = bell_draw(key_of[0], (LAYERS, PATCH_TOK, D), 1.0, 6.0, ((0, 16), (1, 16)))
    image_weight = bell_draw(key_of[1], (LAYERS, D, 3 * D), D ** -0.5, 0.15625, ((0, 16),))
    text_weight = bell_draw(key_of[2], (LAYERS, D, 2 * D), D ** -0.5, 0.15625, ((0, 16), (2, 16)))
    text_states = bell_draw(key_of[3], (LAYERS, TEXT, D), 1.0, 6.0, ((0, 16),))
    stale_cache = jnp.clip(jax.random.uniform(key_of[4], (LAYERS, PATCHES, PATCH_TOK, 2 * D), jnp.float32, -3.0, 3.0) * level_of(key_of[4], (LAYERS, PATCHES, PATCH_TOK, 2 * D), ((0, 16), (2, 16)), -0.4, 0.0), -3.0, 3.0).astype(jnp.bfloat16)
    modulation = bell_draw(key_of[5], (STEPS, LAYERS, 5, D), 1.0, 4.0, ((1, 16),), jnp.float32)
    query_gain = jnp.clip(jnp.exp(math.log(3.0) - 1.7917595 * jax.random.uniform(key_of[6], (LAYERS, HDIM), jnp.float32) ** level_of(key_of[6], (LAYERS, HDIM), ((0, 16),), -0.2, 0.2)), 0.5, 3.0)
    key_gain = jnp.clip(jnp.exp(math.log(3.0) - 1.7917595 * jax.random.uniform(key_of[7], (LAYERS, HDIM), jnp.float32) ** level_of(key_of[7], (LAYERS, HDIM), ((0, 16),), -0.2, 0.2)), 0.5, 3.0)
    text_gain = jnp.clip(jnp.exp(math.log(3.0) - 1.7917595 * jax.random.uniform(key_of[8], (LAYERS, HDIM), jnp.float32) ** level_of(key_of[8], (LAYERS, HDIM), ((0, 16),), -0.2, 0.2)), 0.5, 3.0)
    timestep = plant(jax.random.randint(key_of[9], (LAYERS,), 0, STEPS), jax.random.fold_in(key_of[9], 1), 0, STEPS - 1).astype(jnp.int32)
    layer_patch_index = plant(jax.random.randint(key_of[10], (LAYERS,), 0, PATCHES), jax.random.fold_in(key_of[10], 1), 0, PATCHES - 1).astype(jnp.int32)
    return dict(states=states, image_weight=image_weight, text_weight=text_weight, text_states=text_states, stale_cache=stale_cache, modulation=modulation, query_gain=query_gain, key_gain=key_gain, text_gain=text_gain, timestep=timestep, layer_patch_index=layer_patch_index)


def layer_norm(values):
    center = values - lax.optimization_barrier(jnp.mean(values, axis=-1, keepdims=True))
    return center * lax.rsqrt(lax.optimization_barrier(jnp.mean(center * center, axis=-1, keepdims=True)) + 1e-06)

def head_norm(values, head_gain_table):
    rows_n = values.shape[0]
    size_head = head_gain_table.shape[0]
    per_head = values.reshape(rows_n, -1, size_head)
    scaled = per_head * lax.rsqrt(lax.optimization_barrier(jnp.mean(per_head * per_head, axis=-1, keepdims=True)) + 1e-06) * head_gain_table
    return scaled.reshape(rows_n, -1)

def reference(states, image_weight, text_weight, text_states, stale_cache, modulation, query_gain, key_gain, text_gain, timestep, layer_patch_index):
    attn_width = HEADS * HDIM
    per_layer = jnp.moveaxis(modulation, 1, 0)

    def one_layer(inputs):
        current, weight_img, weight_txt, text_now, memo_present, table_now, asking_multiplier, gain_k, caption_multiplier, slot_now, step_now = inputs
        step_mask = jnp.arange(STEPS, dtype=jnp.int32) == step_now
        modulate = lax.optimization_barrier(jnp.sum(jnp.where(step_mask[:, None, None], table_now, 0.0), axis=0))
        normed = (layer_norm(current.astype(jnp.float32)) * (1.0 + modulate[1]) + modulate[0]).astype(jnp.bfloat16)
        project = jnp.dot(normed, weight_img, preferred_element_type=jnp.float32)
        queries = head_norm(project[:, :attn_width], asking_multiplier).astype(jnp.bfloat16)
        keys_now = head_norm(project[:, attn_width:2 * attn_width], gain_k).astype(jnp.bfloat16)
        values_now = project[:, 2 * attn_width:].astype(jnp.bfloat16)
        fresh = jnp.concatenate([keys_now, values_now], axis=1)
        text_normed = (layer_norm(text_now.astype(jnp.float32)) * (1.0 + modulate[4]) + modulate[3]).astype(jnp.bfloat16)
        text_raw = jnp.dot(text_normed, weight_txt, preferred_element_type=jnp.float32).astype(jnp.bfloat16)
        text_key = head_norm(text_raw[:, :attn_width].astype(jnp.float32), caption_multiplier).astype(jnp.bfloat16)
        text_entries = jnp.concatenate([text_key, text_raw[:, attn_width:]], axis=1)
        slot_mask = jnp.arange(PATCHES, dtype=jnp.int32) == slot_now
        merged = jnp.where(slot_mask[:, None, None], fresh[None], memo_present).reshape(PATCHES * PATCH_TOK, 2 * attn_width)
        entries = jnp.concatenate([text_entries, merged], axis=0)
        asking_channel_lines = queries.reshape(PATCH_TOK, HEADS, HDIM).transpose(1, 0, 2)
        lookup_channel_lines = entries[:, :attn_width].reshape(-1, HEADS, HDIM).transpose(1, 0, 2)
        value_head_rows = entries[:, attn_width:].reshape(-1, HEADS, HDIM).transpose(1, 0, 2)

        def one_head(triple):
            query_h, key_h, value_per_head = triple
            scores = jnp.dot(query_h, key_h.T, preferred_element_type=jnp.float32) * 0.125
            elementwise_powers = jnp.exp(scores)
            weighted = jnp.dot(elementwise_powers.astype(jnp.bfloat16), value_per_head, preferred_element_type=jnp.float32)
            return weighted / lax.optimization_barrier(jnp.sum(elementwise_powers, axis=1, keepdims=True))
        attended = lax.map(one_head, (asking_channel_lines, lookup_channel_lines, value_head_rows))
        attended = attended.transpose(1, 0, 2).reshape(PATCH_TOK, attn_width)
        updated = (current.astype(jnp.float32) + modulate[2] * attended).astype(jnp.bfloat16)
        return (updated, fresh)
    updated, fresh = lax.map(one_layer, (states, image_weight, text_weight, text_states, stale_cache, per_layer, query_gain, key_gain, text_gain, layer_patch_index, timestep))
    return (jnp.roll(updated, 1, axis=0), fresh)
```

```python
import functools

import jax
import jax.numpy as jnp
from jax import lax
from jax.experimental import pallas as pl
from jax.experimental.pallas import tpu as pltpu
from jax.sharding import PartitionSpec as P

MESH = pl.DeviceIdType.MESH
BF = jnp.bfloat16
F32 = jnp.float32

D = 1216
HEADS = 19
HD = 64
TOK = 128
TEXT = 256
BLK = 16
TEXT_COLS = 152
SPARE = 4
ROWS = BLK * TOK
SPARE_ROWS = SPARE * TOK
W_ROWS = 304
SPARE_GROUPS = ((0, 6, 3), (6, 6, 3), (12, 4, 4))
QT = 256


def low_half(rows):
    return lax.broadcasted_iota(jnp.int32, (rows, 128), 1) < HD


def swap_halves(value):
    return pltpu.roll(value, HD, axis=1)


def layer_norm(values):
    center = values - jnp.mean(values, axis=-1, keepdims=True)
    return center * lax.rsqrt(jnp.mean(center * center, axis=-1, keepdims=True) + 1e-06)


def pack_heads(source, sends):
    low = low_half(TOK)

    def tile(index):
        return source[:, 128 * index : 128 * index + 128].astype(F32)

    for head in range(HEADS):
        half = head // 2
        if head % 2 == 0:
            packed = jnp.where(low, tile(half), tile(9 + half))
        else:
            packed = swap_halves(jnp.where(low, tile(10 + half), tile(half)))
        packed = packed.astype(BF)
        if head < BLK:
            sends[head, 0] = packed
        else:
            first, count, _ = SPARE_GROUPS[head - BLK]
            for device in range(first, first + count):
                sends[device, 1] = packed


def kernel(
    sections,
    patch_ref,
    states_hbm,
    weight_hbm,
    text_weight_ref,
    text_hbm,
    stale_hbm,
    mod_ref,
    query_gain_ref,
    key_gain_ref,
    text_gain_ref,
    out_ref,
    fresh_hbm,
    states_v,
    weight_v,
    text_v,
    stale_v,
    entries_v,
    proj_v,
    fresh_v,
    kv_send,
    kv_recv,
    q_send,
    q_recv,
    q_spare,
    q_all,
    acc,
    text_send,
    text_recv,
    text_kv,
    gate_v,
    out_send,
    out_recv,
    prev_v,
    load_sem,
    weight_sem,
    kv_ssem,
    kv_rsem,
    q_ssem,
    q_rsem,
    spare_ssem,
    spare_rsem,
    text_ssem,
    text_ssem2,
    text_rsem,
    out_ssem,
    out_ssem2,
    out_rsem,
    prev_ssem,
    prev_rsem,
    fresh_sem,
):
    sec = lax.axis_index("section")
    me = lax.axis_index("blk")
    after = lax.rem(sec + 1, sections)
    before = lax.rem(sec + sections - 1, sections)

    load_stale = pltpu.make_async_copy(stale_hbm, stale_v, load_sem.at[0])
    load_states = pltpu.make_async_copy(states_hbm, states_v, load_sem.at[1])
    load_text = pltpu.make_async_copy(text_hbm, text_v, load_sem.at[2])
    load_stale.start()
    load_states.start()
    loads = []
    for part in range(D // W_ROWS):
        rows = pl.ds(part * W_ROWS, W_ROWS)
        loads.append(
            pltpu.make_async_copy(weight_hbm.at[rows], weight_v.at[rows], weight_sem.at[part])
        )
        loads[-1].start()
    load_text.start()

    barrier = pltpu.get_barrier_semaphore()

    @pl.loop(1, BLK)
    def _(step):
        pl.semaphore_signal(
            barrier, inc=1, device_id=(sec, lax.rem(me + step, BLK)), device_id_type=MESH
        )

    @pl.loop(0, BLK)
    def _(step):
        pl.semaphore_signal(
            barrier, inc=1, device_id=(before, lax.rem(me + step, BLK)), device_id_type=MESH
        )

    group = jnp.where(me < 6, 0, jnp.where(me < 12, 1, 2))
    per_device = jnp.where(me < 12, 3, 4)
    first_block = (me - 6 * group) * per_device
    spare_head = BLK + group

    def send_entries(kind):
        @pl.loop(1, BLK)
        def _(step):
            to = lax.rem(me + step, BLK)
            pltpu.make_async_remote_copy(
                src_ref=kv_send.at[kind, to],
                dst_ref=kv_recv.at[kind, me],
                send_sem=kv_ssem.at[kind],
                recv_sem=kv_rsem.at[kind, me],
                device_id=(sec, to),
                device_id_type=MESH,
            ).start()

        pltpu.make_async_copy(
            kv_send.at[kind, me], kv_recv.at[kind, me], kv_rsem.at[kind, me]
        ).start()

    load_stale.wait()
    first_worked = patch_ref[0] == 0
    for index in range(HEADS):
        cols = slice(128 * index, 128 * index + 128)
        entries_v[:, cols] = jnp.where(first_worked, stale_v[1, :, cols], stale_v[0, :, cols])
    pack_heads(entries_v, kv_send.at[0])
    pl.semaphore_wait(barrier, 2 * BLK - 1)
    send_entries(0)

    load_states.wait()
    prev_copy = pltpu.make_async_remote_copy(
        src_ref=states_v,
        dst_ref=prev_v,
        send_sem=prev_ssem,
        recv_sem=prev_rsem,
        device_id=(after, me),
        device_id_type=MESH,
    )
    prev_copy.start()

    normed = (
        layer_norm(states_v[...].astype(F32).T) * (1.0 + mod_ref[1:2, :]) + mod_ref[0:1, :]
    ).astype(BF)
    for load in loads:
        load.wait()

    block_ones = (
        (lax.broadcasted_iota(jnp.int32, (128, 128), 0) < HD)
        == (lax.broadcasted_iota(jnp.int32, (128, 128), 1) < HD)
    ).astype(BF)
    query_gain = query_gain_ref[...]
    key_gain = key_gain_ref[...]

    def project(first, last):
        proj_v[:, first:last] = jnp.dot(
            normed, weight_v[:, first:last], preferred_element_type=F32
        )

    def normed_tile(index):
        value = proj_v[:, 128 * index : 128 * index + 128]
        square = value * value
        high = square.astype(BF)
        low = (square - high.astype(F32)).astype(BF)
        mean = (
            jnp.dot(high, block_ones, preferred_element_type=F32)
            + jnp.dot(low, block_ones, preferred_element_type=F32)
        ) * (1.0 / HD)
        gain = jnp.concatenate(
            [
                query_gain if index < 10 else key_gain,
                query_gain if index < 9 else key_gain,
            ],
            axis=1,
        )
        return value * lax.rsqrt(mean + 1e-06) * gain

    low64 = low_half(HD)
    project(0, 1280)
    for index in range(10):
        value = normed_tile(index)
        if index == 9:
            proj_v[:, 128 * index : 128 * index + 128] = value
        top, bottom = value[:HD], value[HD:]
        even = jnp.where(low64, top, swap_halves(bottom))
        q_send[2 * index] = (even.astype(BF).astype(F32) * 0.125).astype(BF)
        if index < 9:
            odd = jnp.where(low64, swap_halves(top), bottom)
            q_send[2 * index + 1] = (odd.astype(BF).astype(F32) * 0.125).astype(BF)

    @pl.loop(1, BLK)
    def _(step):
        to = lax.rem(me + step, BLK)
        pltpu.make_async_remote_copy(
            src_ref=q_send.at[to],
            dst_ref=q_recv.at[me],
            send_sem=q_ssem,
            recv_sem=q_rsem,
            device_id=(sec, to),
            device_id_type=MESH,
        ).start()

    pltpu.make_async_copy(q_send.at[me], q_recv.at[me], q_rsem).start()

    def spare_query(index):
        first, _, size = SPARE_GROUPS[index]
        to = first + me // size
        slot = lax.rem(me, size)
        return to, pltpu.make_async_remote_copy(
            src_ref=q_send.at[BLK + index],
            dst_ref=q_spare.at[slot],
            send_sem=spare_ssem.at[index],
            recv_sem=spare_rsem.at[slot],
            device_id=(sec, to),
            device_id_type=MESH,
        ), pltpu.make_async_copy(
            q_send.at[BLK + index], q_spare.at[slot], spare_rsem.at[slot]
        )

    for index in range(3):
        to, remote, local = spare_query(index)
        pl.when(to != me)(remote.start)
        pl.when(to == me)(local.start)

    project(1280, 2432)
    project(2432, 3648)
    low = low_half(TOK)

    def swapped_tile(index):
        if index == 9 or index >= 19:
            return swap_halves(proj_v[:, 128 * index : 128 * index + 128])
        return swap_halves(normed_tile(index))

    left = swapped_tile(9)
    for index in range(HEADS):
        right = swapped_tile(10 + index)
        fresh_v[:, 128 * index : 128 * index + 128] = jnp.where(low, left, right).astype(BF)
        left = right
    fresh_copy = pltpu.make_async_copy(fresh_v, fresh_hbm, fresh_sem)
    fresh_copy.start()
    pack_heads(fresh_v, kv_send.at[1])
    send_entries(1)

    load_text.wait()
    text_normed = (
        layer_norm(text_v[...].astype(F32).T) * (1.0 + mod_ref[4:5, :]) + mod_ref[3:4, :]
    ).astype(BF)
    text_send[...] = (
        lax.dot_general(
            text_weight_ref[...],
            text_normed,
            (((1,), (1,)), ((), ())),
            preferred_element_type=F32,
        )
        .astype(BF)
        .astype(F32)
    )

    def text_main(step):
        unit = TEXT_COLS // 8 * me + step
        second = unit // TEXT_COLS
        head = (unit - TEXT_COLS * second) // 8
        to_row = pl.multiple_of(HD * second + 8 * lax.rem(unit, 8), 8)
        source = text_send.at[pl.ds(pl.multiple_of(8 * step, 8), 8)]
        target = text_recv.at[0, pl.ds(to_row, 8)]
        return (
            head,
            lambda: pltpu.make_async_remote_copy(
                src_ref=source,
                dst_ref=target,
                send_sem=text_ssem.at[step],
                recv_sem=text_rsem.at[0],
                device_id=(sec, head),
                device_id_type=MESH,
            ),
            lambda: pltpu.make_async_copy(source, target, text_rsem.at[0]),
        )

    @pl.loop(0, TEXT_COLS // 8)
    def _(step):
        head, remote, local = text_main(step)

        @pl.when(jnp.logical_and(head < BLK, head != me))
        def _():
            remote().start()

        @pl.when(head == me)
        def _():
            local().start()

    pieces = ((6, 112, 40, 0, 0), (7, 0, 24, 0, 40), (7, 24, 64, 1, 0), (7, 88, 64, 2, 0))
    second_half = me // 8

    def text_spare(number, step):
        _, row, rows, index, to_row = pieces[number]
        to = SPARE_GROUPS[index][0] + step
        source = text_send.at[pl.ds(row, rows)]
        target = text_recv.at[1, pl.ds(pl.multiple_of(HD * second_half + to_row, 8), rows)]
        return (
            to,
            lambda: pltpu.make_async_remote_copy(
                src_ref=source,
                dst_ref=target,
                send_sem=text_ssem2.at[number, step],
                recv_sem=text_rsem.at[1],
                device_id=(sec, to),
                device_id_type=MESH,
            ),
            lambda: pltpu.make_async_copy(source, target, text_rsem.at[1]),
        )

    for number in range(4):

        @pl.when(lax.rem(me, 8) == pieces[number][0])
        def _():
            @pl.loop(0, SPARE_GROUPS[pieces[number][3]][1])
            def _(step):
                to, remote, local = text_spare(number, step)

                @pl.when(to != me)
                def _():
                    remote().start()

                @pl.when(to == me)
                def _():
                    local().start()

    one = jnp.ones((1, 128), F32)
    low1 = low_half(1)
    gate_pad = jnp.concatenate([mod_ref[2:3, :], jnp.zeros((1, 64), F32)], axis=1)
    for head in range(HEADS):
        gate = gate_pad[:, 128 * (head // 2) : 128 * (head // 2) + 128]
        if head % 2 == 0:
            gate = swap_halves(jnp.broadcast_to(gate, (8, 128)))[0:1]
        gate_v[head : head + 1, :] = jnp.where(low1, one, gate)

    pltpu.make_async_copy(q_recv, q_recv, q_rsem).wait()

    def spread_queries(packed, row):
        value = packed.astype(F32)
        zero = jnp.zeros_like(value)
        q_all[pl.ds(row, HD)] = jnp.where(low64, value, zero).astype(BF)
        q_all[pl.ds(row + HD, HD)] = jnp.where(low64, swap_halves(value), zero).astype(BF)

    @pl.loop(0, BLK)
    def _(step):
        spread_queries(q_recv[step], pl.multiple_of(step * TOK, TOK))

    q_all[pl.ds(ROWS, SPARE_ROWS)] = jnp.zeros((SPARE_ROWS, 128), BF)
    for slot in range(SPARE):

        @pl.when(jnp.logical_and(slot < per_device, first_block + slot < BLK))
        def _():
            pltpu.make_async_copy(q_spare.at[slot], q_spare.at[slot], spare_rsem.at[slot]).wait()
            spread_queries(q_spare[slot], ROWS + slot * TOK)

    low256 = low_half(256)

    def attend(entries, first, rows):
        values = jnp.where(low256, jnp.ones((256, 128), F32), entries.astype(F32)).astype(BF)

        @pl.loop(0, rows // QT)
        def _(step):
            at = pl.ds(pl.multiple_of(first + step * QT, QT), QT)
            scores = lax.dot_general(
                q_all[at], entries, (((1,), (1,)), ((), ())), preferred_element_type=F32
            )
            powers = jnp.exp(scores).astype(BF)
            acc[at] += jnp.dot(powers, values, preferred_element_type=F32)

    acc[...] = jnp.zeros_like(acc)

    def attend_patch(kind):
        @pl.loop(0, BLK // 2)
        def _(step):
            pair = lax.rem(me // 2 + BLK // 2 - step, BLK // 2)
            for core in range(2):
                one_source = kv_recv.at[kind, 2 * pair + core]
                pltpu.make_async_copy(
                    one_source, one_source, kv_rsem.at[kind, 2 * pair + core]
                ).wait()
            for which, first, rows in ((0, 0, ROWS), (1, ROWS, SPARE_ROWS)):
                entries = kv_recv[kind, pl.ds(2 * pair, 2), which].reshape(256, 128)
                attend(entries, first, rows)

    attend_patch(0)

    text_gain = jnp.concatenate([text_gain_ref[...], jnp.ones((1, HD), F32)], axis=1)
    for which, first, rows in ((0, 0, ROWS), (1, ROWS, SPARE_ROWS)):
        pltpu.make_async_copy(
            text_recv.at[which], text_recv.at[which], text_rsem.at[which]
        ).wait()
        value = text_recv[which].T
        square = jnp.where(low256, value * value, 0.0)
        mean = jnp.sum(square, axis=1, keepdims=True) * (1.0 / HD)
        scaled = value * lax.rsqrt(mean + 1e-06) * text_gain
        text_kv[which] = jnp.where(low256, scaled, value).astype(BF)
        attend(text_kv[which], first, rows)

    attend_patch(1)

    def result_of(row, head):
        value = acc[pl.ds(row, TOK)] * gate_v[pl.ds(head, 1), :]
        turned = value.T
        return (turned[HD:] / turned[:HD]).astype(BF)

    def result_copy(slot, head, block, sem):
        return pltpu.make_async_remote_copy(
            src_ref=out_send.at[slot],
            dst_ref=out_recv.at[head],
            send_sem=sem,
            recv_sem=out_rsem,
            device_id=(after, block),
            device_id_type=MESH,
        )

    @pl.loop(0, BLK)
    def _(step):
        block = lax.rem(me + step, BLK)
        out_send[block] = result_of(pl.multiple_of(block * TOK, TOK), me)
        result_copy(block, me, block, out_ssem).start()

    for slot in range(SPARE):

        @pl.when(jnp.logical_and(slot < per_device, first_block + slot < BLK))
        def _():
            out_send[BLK + slot] = result_of(ROWS + slot * TOK, spare_head)
            result_copy(BLK + slot, spare_head, first_block + slot, out_ssem2.at[slot]).start()

    prev_copy.wait_recv()
    pltpu.make_async_copy(out_recv, out_recv, out_rsem).wait()
    for head in range(HEADS):
        rows = slice(HD * head, HD * head + HD)
        out_ref[rows, :] = (prev_v[rows, :].astype(F32) + out_recv[head].astype(F32)).astype(BF)

    fresh_copy.wait()
    prev_copy.wait_send()
    for kind in range(2):
        sent = kv_send.at[kind, pl.ds(0, BLK - 1)]
        pltpu.make_async_copy(sent, sent, kv_ssem.at[kind]).wait()
    sent = q_send.at[pl.ds(0, BLK - 1)]
    pltpu.make_async_copy(sent, sent, q_ssem).wait()
    for index in range(3):
        to, remote, _ = spare_query(index)
        pl.when(to != me)(remote.wait_send)

    @pl.loop(0, TEXT_COLS // 8)
    def _(step):
        head, remote, _ = text_main(step)

        @pl.when(jnp.logical_and(head < BLK, head != me))
        def _():
            remote().wait_send()

    for number in range(4):

        @pl.when(lax.rem(me, 8) == pieces[number][0])
        def _():
            @pl.loop(0, SPARE_GROUPS[pieces[number][3]][1])
            def _(step):
                to, remote, _ = text_spare(number, step)

                @pl.when(to != me)
                def _():
                    remote().wait_send()

    sent = out_send.at[pl.ds(0, BLK)]
    pltpu.make_async_copy(sent, sent, out_ssem).wait()
    for slot in range(SPARE):

        @pl.when(jnp.logical_and(slot < per_device, first_block + slot < BLK))
        def _():
            result_copy(BLK + slot, spare_head, first_block + slot, out_ssem2.at[slot]).wait_send()


def body(
    sections,
    states,
    image_weight,
    text_weight,
    text_states,
    stale_cache,
    modulation,
    query_gain,
    key_gain,
    text_gain,
    timestep,
    layer_patch_index,
):
    modulate = lax.dynamic_index_in_dim(modulation[:, 0], timestep[0], 0, keepdims=False)
    vmem = pl.BlockSpec(memory_space=pltpu.VMEM)
    anywhere = pl.BlockSpec(memory_space=pl.ANY)
    dma = pltpu.SemaphoreType.DMA
    next_states, fresh = pl.pallas_call(
        functools.partial(kernel, sections),
        out_shape=(
            jax.ShapeDtypeStruct((D, TOK), BF),
            jax.ShapeDtypeStruct((TOK, 2 * D), BF),
        ),
        in_specs=[
            pl.BlockSpec(memory_space=pltpu.SMEM),
            anywhere,
            anywhere,
            vmem,
            anywhere,
            anywhere,
            vmem,
            vmem,
            vmem,
            vmem,
        ],
        out_specs=(vmem, anywhere),
        scratch_shapes=[
            pltpu.VMEM((D, TOK), BF),
            pltpu.VMEM((D, 3 * D), BF),
            pltpu.VMEM((D, TEXT), BF),
            pltpu.VMEM((2, TOK, 2 * D), BF),
            pltpu.VMEM((TOK, 2 * D), BF),
            pltpu.VMEM((TOK, 3 * D + 64), F32),
            pltpu.VMEM((TOK, 2 * D), BF),
            pltpu.VMEM((2, BLK, 2, TOK, 128), BF),
            pltpu.VMEM((2, BLK, 2, TOK, 128), BF),
            pltpu.VMEM((HEADS, HD, 128), BF),
            pltpu.VMEM((BLK, HD, 128), BF),
            pltpu.VMEM((SPARE, HD, 128), BF),
            pltpu.VMEM((ROWS + SPARE_ROWS, 128), BF),
            pltpu.VMEM((ROWS + SPARE_ROWS, 128), F32),
            pltpu.VMEM((TEXT_COLS, TEXT), F32),
            pltpu.VMEM((2, 128, TEXT), F32),
            pltpu.VMEM((2, TEXT, 128), BF),
            pltpu.VMEM((24, 128), F32),
            pltpu.VMEM((BLK + SPARE, HD, 128), BF),
            pltpu.VMEM((HEADS, HD, 128), BF),
            pltpu.VMEM((D, TOK), BF),
            dma((3,)),
            dma((D // W_ROWS,)),
            dma((2,)),
            dma((2, BLK)),
            dma,
            dma,
            dma((3,)),
            dma((SPARE,)),
            dma((TEXT_COLS // 8,)),
            dma((4, 6)),
            dma((2,)),
            dma,
            dma((SPARE,)),
            dma,
            dma,
            dma,
            dma,
        ],
        compiler_params=pltpu.CompilerParams(
            collective_id=0, has_side_effects=True, vmem_limit_bytes=56 * 1024 * 1024
        ),
    )(
        layer_patch_index,
        jnp.swapaxes(states[0], 0, 1),
        image_weight[0],
        jnp.swapaxes(text_weight[0], 0, 1),
        jnp.swapaxes(text_states[0], 0, 1),
        stale_cache[0],
        modulate,
        query_gain,
        key_gain,
        text_gain,
    )
    return (jnp.swapaxes(next_states, 0, 1)[None], fresh[None])


def solution(mesh):
    in_specs = (
        P("section", "blk", None),
        P("section", None, None),
        P("section", None, "blk"),
        P("section", None, None),
        P("section", None, "blk", None),
        P(None, "section", None, None),
        P("section", None),
        P("section", None),
        P("section", None),
        P("section"),
        P("section"),
    )
    out_specs = (P("section", "blk", None), P("section", "blk", None))
    return jax.shard_map(
        functools.partial(body, mesh.shape["section"]),
        mesh=mesh,
        in_specs=in_specs,
        out_specs=out_specs,
        check_vma=False,
    )
```

```python
import functools

import jax
import jax.numpy as jnp
from jax import lax
from jax.experimental import pallas as pl
from jax.experimental.pallas import tpu as pltpu
from jax.sharding import PartitionSpec as P

MESH = pl.DeviceIdType.MESH
BF = jnp.bfloat16
F32 = jnp.float32

D = 1216
HEADS = 19
HD = 64
TOK = 128
TEXT = 256
BLK = 16
TEXT_COLS = 152
SPARE = 4
ROWS = BLK * TOK
SPARE_ROWS = SPARE * TOK
W_ROWS = 304
SPARE_GROUPS = ((0, 6, 3), (6, 6, 3), (12, 4, 4))
QT = 512


def low_half(rows):
    return lax.broadcasted_iota(jnp.int32, (rows, 128), 1) < HD


def swap_halves(value):
    return pltpu.roll(value, HD, axis=1)


def layer_norm(values):
    center = values - jnp.mean(values, axis=-1, keepdims=True)
    return center * lax.rsqrt(jnp.mean(center * center, axis=-1, keepdims=True) + 1e-06)


def pack_heads(source, sends):
    low = low_half(TOK)

    def tile(index):
        return source[:, 128 * index : 128 * index + 128].astype(F32)

    for head in range(HEADS):
        half = head // 2
        if head % 2 == 0:
            packed = jnp.where(low, tile(half), tile(9 + half))
        else:
            packed = swap_halves(jnp.where(low, tile(10 + half), tile(half)))
        packed = packed.astype(BF)
        if head < BLK:
            sends[head, 0] = packed
        else:
            first, count, _ = SPARE_GROUPS[head - BLK]
            for device in range(first, first + count):
                sends[device, 1] = packed


def kernel(
    sections,
    patch_ref,
    states_hbm,
    weight_hbm,
    text_weight_ref,
    text_hbm,
    stale_hbm,
    mod_ref,
    query_gain_ref,
    key_gain_ref,
    text_gain_ref,
    out_ref,
    fresh_hbm,
    states_v,
    weight_v,
    text_v,
    stale_v,
    entries_v,
    proj_v,
    fresh_v,
    kv_send,
    kv_recv,
    q_send,
    q_recv,
    q_spare,
    q_all,
    acc,
    text_send,
    text_recv,
    gate_v,
    out_send,
    out_recv,
    prev_v,
    load_sem,
    weight_sem,
    kv_ssem,
    kv_rsem,
    q_ssem,
    q_rsem,
    spare_ssem,
    spare_rsem,
    text_ssem,
    text_ssem2,
    text_rsem,
    out_ssem,
    out_ssem2,
    out_rsem,
    prev_ssem,
    prev_rsem,
    fresh_sem,
):
    sec = lax.axis_index("section")
    me = lax.axis_index("blk")
    after = lax.rem(sec + 1, sections)
    before = lax.rem(sec + sections - 1, sections)

    load_stale = pltpu.make_async_copy(stale_hbm, stale_v, load_sem.at[0])
    load_states = pltpu.make_async_copy(states_hbm, states_v, load_sem.at[1])
    load_text = pltpu.make_async_copy(text_hbm, text_v, load_sem.at[2])
    load_stale.start()
    load_states.start()
    loads = []
    for part in range(D // W_ROWS):
        rows = pl.ds(part * W_ROWS, W_ROWS)
        loads.append(
            pltpu.make_async_copy(weight_hbm.at[rows], weight_v.at[rows], weight_sem.at[part])
        )
        loads[-1].start()
    load_text.start()

    barrier = pltpu.get_barrier_semaphore()

    @pl.loop(1, BLK)
    def _(step):
        pl.semaphore_signal(
            barrier, inc=1, device_id=(sec, lax.rem(me + step, BLK)), device_id_type=MESH
        )

    @pl.loop(0, BLK)
    def _(step):
        pl.semaphore_signal(
            barrier, inc=1, device_id=(before, lax.rem(me + step, BLK)), device_id_type=MESH
        )

    group = jnp.where(me < 6, 0, jnp.where(me < 12, 1, 2))
    per_device = jnp.where(me < 12, 3, 4)
    first_block = (me - 6 * group) * per_device
    spare_head = BLK + group

    def send_entries(kind):
        @pl.loop(1, BLK)
        def _(step):
            to = lax.rem(me + step, BLK)
            pltpu.make_async_remote_copy(
                src_ref=kv_send.at[kind, to],
                dst_ref=kv_recv.at[kind, :, me],
                send_sem=kv_ssem.at[kind],
                recv_sem=kv_rsem.at[kind, me],
                device_id=(sec, to),
                device_id_type=MESH,
            ).start()

        pltpu.make_async_copy(
            kv_send.at[kind, me], kv_recv.at[kind, :, me], kv_rsem.at[kind, me]
        ).start()

    load_stale.wait()
    first_worked = patch_ref[0] == 0
    for index in range(HEADS):
        cols = slice(128 * index, 128 * index + 128)
        entries_v[:, cols] = jnp.where(first_worked, stale_v[1, :, cols], stale_v[0, :, cols])
    pack_heads(entries_v, kv_send.at[0])
    pl.semaphore_wait(barrier, 2 * BLK - 1)
    send_entries(0)

    load_states.wait()
    prev_copy = pltpu.make_async_remote_copy(
        src_ref=states_v,
        dst_ref=prev_v,
        send_sem=prev_ssem,
        recv_sem=prev_rsem,
        device_id=(after, me),
        device_id_type=MESH,
    )
    prev_copy.start()

    normed = (
        layer_norm(states_v[...].astype(F32).T) * (1.0 + mod_ref[1:2, :]) + mod_ref[0:1, :]
    ).astype(BF)
    for load in loads:
        load.wait()

    block_ones = (
        (lax.broadcasted_iota(jnp.int32, (128, 128), 0) < HD)
        == (lax.broadcasted_iota(jnp.int32, (128, 128), 1) < HD)
    ).astype(BF)
    query_gain = query_gain_ref[...]
    key_gain = key_gain_ref[...]

    def project(first, last):
        proj_v[:, first:last] = jnp.dot(
            normed, weight_v[:, first:last], preferred_element_type=F32
        )

    def normed_tile(index):
        value = proj_v[:, 128 * index : 128 * index + 128]
        square = value * value
        high = square.astype(BF)
        low = (square - high.astype(F32)).astype(BF)
        mean = (
            jnp.dot(high, block_ones, preferred_element_type=F32)
            + jnp.dot(low, block_ones, preferred_element_type=F32)
        ) * (1.0 / HD)
        gain = jnp.concatenate(
            [
                query_gain if index < 10 else key_gain,
                query_gain if index < 9 else key_gain,
            ],
            axis=1,
        )
        return value * lax.rsqrt(mean + 1e-06) * gain

    low64 = low_half(HD)
    project(0, 1280)
    for index in range(10):
        value = normed_tile(index)
        if index == 9:
            proj_v[:, 128 * index : 128 * index + 128] = value
        top, bottom = value[:HD], value[HD:]
        even = jnp.where(low64, top, swap_halves(bottom))
        q_send[2 * index] = (even.astype(BF).astype(F32) * 0.125).astype(BF)
        if index < 9:
            odd = jnp.where(low64, swap_halves(top), bottom)
            q_send[2 * index + 1] = (odd.astype(BF).astype(F32) * 0.125).astype(BF)

    @pl.loop(1, BLK)
    def _(step):
        to = lax.rem(me + step, BLK)
        pltpu.make_async_remote_copy(
            src_ref=q_send.at[to],
            dst_ref=q_recv.at[me],
            send_sem=q_ssem,
            recv_sem=q_rsem,
            device_id=(sec, to),
            device_id_type=MESH,
        ).start()

    pltpu.make_async_copy(q_send.at[me], q_recv.at[me], q_rsem).start()

    def spare_query(index):
        first, _, size = SPARE_GROUPS[index]
        to = first + me // size
        slot = lax.rem(me, size)
        return to, pltpu.make_async_remote_copy(
            src_ref=q_send.at[BLK + index],
            dst_ref=q_spare.at[slot],
            send_sem=spare_ssem.at[index],
            recv_sem=spare_rsem.at[slot],
            device_id=(sec, to),
            device_id_type=MESH,
        ), pltpu.make_async_copy(
            q_send.at[BLK + index], q_spare.at[slot], spare_rsem.at[slot]
        )

    for index in range(3):
        to, remote, local = spare_query(index)
        pl.when(to != me)(remote.start)
        pl.when(to == me)(local.start)

    project(1280, 2432)
    project(2432, 3648)
    low = low_half(TOK)

    def swapped_tile(index):
        if index == 9 or index >= 19:
            return swap_halves(proj_v[:, 128 * index : 128 * index + 128])
        return swap_halves(normed_tile(index))

    left = swapped_tile(9)
    for index in range(HEADS):
        right = swapped_tile(10 + index)
        fresh_v[:, 128 * index : 128 * index + 128] = jnp.where(low, left, right).astype(BF)
        left = right
    fresh_copy = pltpu.make_async_copy(fresh_v, fresh_hbm, fresh_sem)
    fresh_copy.start()
    pack_heads(fresh_v, kv_send.at[1])
    send_entries(1)

    load_text.wait()
    text_normed = (
        layer_norm(text_v[...].astype(F32).T) * (1.0 + mod_ref[4:5, :]) + mod_ref[3:4, :]
    ).astype(BF)
    text_send[...] = (
        lax.dot_general(
            text_weight_ref[...],
            text_normed,
            (((1,), (1,)), ((), ())),
            preferred_element_type=F32,
        )
        .astype(BF)
        .astype(F32)
    )

    def text_main(step):
        unit = TEXT_COLS // 8 * me + step
        second = unit // TEXT_COLS
        head = (unit - TEXT_COLS * second) // 8
        to_row = pl.multiple_of(HD * second + 8 * lax.rem(unit, 8), 8)
        source = text_send.at[pl.ds(pl.multiple_of(8 * step, 8), 8)]
        target = text_recv.at[0, pl.ds(to_row, 8)]
        return (
            head,
            lambda: pltpu.make_async_remote_copy(
                src_ref=source,
                dst_ref=target,
                send_sem=text_ssem.at[step],
                recv_sem=text_rsem.at[0],
                device_id=(sec, head),
                device_id_type=MESH,
            ),
            lambda: pltpu.make_async_copy(source, target, text_rsem.at[0]),
        )

    @pl.loop(0, TEXT_COLS // 8)
    def _(step):
        head, remote, local = text_main(step)

        @pl.when(jnp.logical_and(head < BLK, head != me))
        def _():
            remote().start()

        @pl.when(head == me)
        def _():
            local().start()

    pieces = ((6, 112, 40, 0, 0), (7, 0, 24, 0, 40), (7, 24, 64, 1, 0), (7, 88, 64, 2, 0))
    second_half = me // 8

    def text_spare(number, step):
        _, row, rows, index, to_row = pieces[number]
        to = SPARE_GROUPS[index][0] + step
        source = text_send.at[pl.ds(row, rows)]
        target = text_recv.at[1, pl.ds(pl.multiple_of(HD * second_half + to_row, 8), rows)]
        return (
            to,
            lambda: pltpu.make_async_remote_copy(
                src_ref=source,
                dst_ref=target,
                send_sem=text_ssem2.at[number, step],
                recv_sem=text_rsem.at[1],
                device_id=(sec, to),
                device_id_type=MESH,
            ),
            lambda: pltpu.make_async_copy(source, target, text_rsem.at[1]),
        )

    for number in range(4):

        @pl.when(lax.rem(me, 8) == pieces[number][0])
        def _():
            @pl.loop(0, SPARE_GROUPS[pieces[number][3]][1])
            def _(step):
                to, remote, local = text_spare(number, step)

                @pl.when(to != me)
                def _():
                    remote().start()

                @pl.when(to == me)
                def _():
                    local().start()

    one = jnp.ones((1, 128), F32)
    low1 = low_half(1)
    gate_pad = jnp.concatenate([mod_ref[2:3, :], jnp.zeros((1, 64), F32)], axis=1)
    for head in range(HEADS):
        gate = gate_pad[:, 128 * (head // 2) : 128 * (head // 2) + 128]
        if head % 2 == 0:
            gate = swap_halves(jnp.broadcast_to(gate, (8, 128)))[0:1]
        gate_v[head : head + 1, :] = jnp.where(low1, one, gate)

    pltpu.make_async_copy(q_recv, q_recv, q_rsem).wait()

    def spread_queries(packed, row):
        value = packed.astype(F32)
        zero = jnp.zeros_like(value)
        q_all[pl.ds(row, HD)] = jnp.where(low64, value, zero).astype(BF)
        q_all[pl.ds(row + HD, HD)] = jnp.where(low64, swap_halves(value), zero).astype(BF)

    @pl.loop(0, BLK)
    def _(step):
        spread_queries(q_recv[step], pl.multiple_of(step * TOK, TOK))

    q_all[pl.ds(ROWS, SPARE_ROWS)] = jnp.zeros((SPARE_ROWS, 128), BF)
    for slot in range(SPARE):

        @pl.when(jnp.logical_and(slot < per_device, first_block + slot < BLK))
        def _():
            pltpu.make_async_copy(q_spare.at[slot], q_spare.at[slot], spare_rsem.at[slot]).wait()
            spread_queries(q_spare[slot], ROWS + slot * TOK)

    def attend(kind, which, first, rows, sources):
        entries = kv_recv[kind, which, 0:sources].reshape(sources * TOK, 128)
        values = jnp.where(
            low_half(sources * TOK), jnp.ones(entries.shape, F32), entries.astype(F32)
        ).astype(BF)

        @pl.loop(0, rows // QT)
        def _(step):
            at = pl.ds(pl.multiple_of(first + step * QT, QT), QT)
            scores = lax.dot_general(
                q_all[at], entries, (((1,), (1,)), ((), ())), preferred_element_type=F32
            )
            powers = jnp.exp(scores).astype(BF)
            sums = jnp.dot(powers, values, preferred_element_type=F32)
            if kind == 0:
                acc[at] = sums
            else:
                acc[at] += sums

    def wait_entries(kind):
        @pl.loop(0, BLK)
        def _(source):
            block = kv_recv.at[kind, :, source]
            pltpu.make_async_copy(block, block, kv_rsem.at[kind, source]).wait()

    wait_entries(0)
    for which, first, rows in ((0, 0, ROWS), (1, ROWS, SPARE_ROWS)):
        attend(0, which, first, rows, BLK)

    low256 = low_half(TEXT)
    text_gain = jnp.concatenate([text_gain_ref[...], jnp.ones((1, HD), F32)], axis=1)
    for which in range(2):
        pltpu.make_async_copy(
            text_recv.at[which], text_recv.at[which], text_rsem.at[which]
        ).wait()
        value = text_recv[which].T
        square = jnp.where(low256, value * value, 0.0)
        mean = jnp.sum(square, axis=1, keepdims=True) * (1.0 / HD)
        scaled = value * lax.rsqrt(mean + 1e-06) * text_gain
        text_entries = jnp.where(low256, scaled, value).astype(BF)
        kv_recv[1, which, BLK : BLK + 2] = text_entries.reshape(2, TOK, 128)

    wait_entries(1)
    for which, first, rows in ((0, 0, ROWS), (1, ROWS, SPARE_ROWS)):
        attend(1, which, first, rows, BLK + 2)

    def result_of(row, head):
        value = acc[pl.ds(row, TOK)] * gate_v[pl.ds(head, 1), :]
        turned = value.T
        return (turned[HD:] / turned[:HD]).astype(BF)

    def result_copy(slot, head, block, sem):
        return pltpu.make_async_remote_copy(
            src_ref=out_send.at[slot],
            dst_ref=out_recv.at[head],
            send_sem=sem,
            recv_sem=out_rsem,
            device_id=(after, block),
            device_id_type=MESH,
        )

    @pl.loop(0, BLK)
    def _(step):
        block = lax.rem(me + step, BLK)
        out_send[block] = result_of(pl.multiple_of(block * TOK, TOK), me)
        result_copy(block, me, block, out_ssem).start()

    for slot in range(SPARE):

        @pl.when(jnp.logical_and(slot < per_device, first_block + slot < BLK))
        def _():
            out_send[BLK + slot] = result_of(ROWS + slot * TOK, spare_head)
            result_copy(BLK + slot, spare_head, first_block + slot, out_ssem2.at[slot]).start()

    prev_copy.wait_recv()
    pltpu.make_async_copy(out_recv, out_recv, out_rsem).wait()
    for head in range(HEADS):
        rows = slice(HD * head, HD * head + HD)
        out_ref[rows, :] = (prev_v[rows, :].astype(F32) + out_recv[head].astype(F32)).astype(BF)

    fresh_copy.wait()
    prev_copy.wait_send()
    for kind in range(2):
        sent = kv_send.at[kind, pl.ds(0, BLK - 1)]
        pltpu.make_async_copy(sent, sent, kv_ssem.at[kind]).wait()
    sent = q_send.at[pl.ds(0, BLK - 1)]
    pltpu.make_async_copy(sent, sent, q_ssem).wait()
    for index in range(3):
        to, remote, _ = spare_query(index)
        pl.when(to != me)(remote.wait_send)

    @pl.loop(0, TEXT_COLS // 8)
    def _(step):
        head, remote, _ = text_main(step)

        @pl.when(jnp.logical_and(head < BLK, head != me))
        def _():
            remote().wait_send()

    for number in range(4):

        @pl.when(lax.rem(me, 8) == pieces[number][0])
        def _():
            @pl.loop(0, SPARE_GROUPS[pieces[number][3]][1])
            def _(step):
                to, remote, _ = text_spare(number, step)

                @pl.when(to != me)
                def _():
                    remote().wait_send()

    sent = out_send.at[pl.ds(0, BLK)]
    pltpu.make_async_copy(sent, sent, out_ssem).wait()
    for slot in range(SPARE):

        @pl.when(jnp.logical_and(slot < per_device, first_block + slot < BLK))
        def _():
            result_copy(BLK + slot, spare_head, first_block + slot, out_ssem2.at[slot]).wait_send()


def body(
    sections,
    states,
    image_weight,
    text_weight,
    text_states,
    stale_cache,
    modulation,
    query_gain,
    key_gain,
    text_gain,
    timestep,
    layer_patch_index,
):
    modulate = lax.dynamic_index_in_dim(modulation[:, 0], timestep[0], 0, keepdims=False)
    vmem = pl.BlockSpec(memory_space=pltpu.VMEM)
    anywhere = pl.BlockSpec(memory_space=pl.ANY)
    dma = pltpu.SemaphoreType.DMA
    next_states, fresh = pl.pallas_call(
        functools.partial(kernel, sections),
        out_shape=(
            jax.ShapeDtypeStruct((D, TOK), BF),
            jax.ShapeDtypeStruct((TOK, 2 * D), BF),
        ),
        in_specs=[
            pl.BlockSpec(memory_space=pltpu.SMEM),
            anywhere,
            anywhere,
            vmem,
            anywhere,
            anywhere,
            vmem,
            vmem,
            vmem,
            vmem,
        ],
        out_specs=(vmem, anywhere),
        scratch_shapes=[
            pltpu.VMEM((D, TOK), BF),
            pltpu.VMEM((D, 3 * D), BF),
            pltpu.VMEM((D, TEXT), BF),
            pltpu.VMEM((2, TOK, 2 * D), BF),
            pltpu.VMEM((TOK, 2 * D), BF),
            pltpu.VMEM((TOK, 3 * D + 64), F32),
            pltpu.VMEM((TOK, 2 * D), BF),
            pltpu.VMEM((2, BLK, 2, TOK, 128), BF),
            pltpu.VMEM((2, 2, BLK + 2, TOK, 128), BF),
            pltpu.VMEM((HEADS, HD, 128), BF),
            pltpu.VMEM((BLK, HD, 128), BF),
            pltpu.VMEM((SPARE, HD, 128), BF),
            pltpu.VMEM((ROWS + SPARE_ROWS, 128), BF),
            pltpu.VMEM((ROWS + SPARE_ROWS, 128), F32),
            pltpu.VMEM((TEXT_COLS, TEXT), F32),
            pltpu.VMEM((2, 128, TEXT), F32),
            pltpu.VMEM((24, 128), F32),
            pltpu.VMEM((BLK + SPARE, HD, 128), BF),
            pltpu.VMEM((HEADS, HD, 128), BF),
            pltpu.VMEM((D, TOK), BF),
            dma((3,)),
            dma((D // W_ROWS,)),
            dma((2,)),
            dma((2, BLK)),
            dma,
            dma,
            dma((3,)),
            dma((SPARE,)),
            dma((TEXT_COLS // 8,)),
            dma((4, 6)),
            dma((2,)),
            dma,
            dma((SPARE,)),
            dma,
            dma,
            dma,
            dma,
        ],
        compiler_params=pltpu.CompilerParams(
            collective_id=0, has_side_effects=True, vmem_limit_bytes=56 * 1024 * 1024
        ),
    )(
        layer_patch_index,
        jnp.swapaxes(states[0], 0, 1),
        image_weight[0],
        jnp.swapaxes(text_weight[0], 0, 1),
        jnp.swapaxes(text_states[0], 0, 1),
        stale_cache[0],
        modulate,
        query_gain,
        key_gain,
        text_gain,
    )
    return (jnp.swapaxes(next_states, 0, 1)[None], fresh[None])


def solution(mesh):
    in_specs = (
        P("section", "blk", None),
        P("section", None, None),
        P("section", None, "blk"),
        P("section", None, None),
        P("section", None, "blk", None),
        P(None, "section", None, None),
        P("section", None),
        P("section", None),
        P("section", None),
        P("section"),
        P("section"),
    )
    out_specs = (P("section", "blk", None), P("section", "blk", None))
    return jax.shard_map(
        functools.partial(body, mesh.shape["section"]),
        mesh=mesh,
        in_specs=in_specs,
        out_specs=out_specs,
        check_vma=False,
    )
```

```python
import functools

import jax
import jax.numpy as jnp
from jax import lax
from jax.experimental import pallas as pl
from jax.experimental.pallas import tpu as pltpu
from jax.sharding import PartitionSpec as P

MESH = pl.DeviceIdType.MESH
BF = jnp.bfloat16
F32 = jnp.float32

D = 1216
HEADS = 19
HD = 64
TOK = 128
TEXT = 256
BLK = 16
TEXT_COLS = 152
SPARE = 4
ROWS = BLK * TOK
SPARE_ROWS = SPARE * TOK
W_ROWS = 304
SPARE_DEVICES = 4
SPARE_HEADS = 3
QT = 512


def low_half(rows):
    return lax.broadcasted_iota(jnp.int32, (rows, 128), 1) < HD


def swap_halves(value):
    return pltpu.roll(value, HD, axis=1)


def layer_norm(values):
    center = values - jnp.mean(values, axis=-1, keepdims=True)
    return center * lax.rsqrt(jnp.mean(center * center, axis=-1, keepdims=True) + 1e-06)


def pack_heads(source, mains, spares):
    low = low_half(TOK)

    def tile(index):
        return source[:, 128 * index : 128 * index + 128].astype(F32)

    for head in range(HEADS):
        half = head // 2
        if head % 2 == 0:
            packed = jnp.where(low, tile(half), tile(9 + half))
        else:
            packed = swap_halves(jnp.where(low, tile(10 + half), tile(half)))
        if head < BLK:
            mains[head] = packed.astype(BF)
        else:
            spares[head - BLK] = packed.astype(BF)


def kernel(
    sections,
    patch_ref,
    step_ref,
    states_hbm,
    weight_hbm,
    text_weight_ref,
    text_hbm,
    stale_hbm,
    mod_hbm,
    query_gain_ref,
    key_gain_ref,
    text_gain_ref,
    out_hbm,
    fresh_hbm,
    states_v,
    weight_v,
    text_v,
    stale_v,
    mod_v,
    entries_v,
    proj_v,
    fresh_v,
    main_send,
    main_recv,
    spare_send,
    spare_recv,
    q_send,
    q_recv,
    q_spare,
    q_all,
    state_recv,
    state_spare,
    acc,
    text_send,
    text_recv,
    gate_v,
    out_send,
    load_sem,
    weight_sem,
    main_ssem,
    main_rsem,
    spare_ssem,
    spare_rsem,
    pass_ssem,
    pass_rsem,
    q_ssem,
    q_rsem,
    q_ssem2,
    q_rsem2,
    state_ssem,
    state_rsem,
    state_ssem2,
    state_rsem2,
    text_ssem,
    text_ssem2,
    text_rsem,
    out_ssem,
    out_ssem2,
    out_rsem,
    fresh_sem,
):
    sec = lax.axis_index("section")
    me = lax.axis_index("blk")
    after = lax.rem(sec + 1, sections)
    before = lax.rem(sec + sections - 1, sections)

    load_stale = pltpu.make_async_copy(stale_hbm, stale_v, load_sem.at[0])
    load_states = pltpu.make_async_copy(states_hbm, states_v, load_sem.at[1])
    load_text = pltpu.make_async_copy(text_hbm, text_v, load_sem.at[2])
    load_mod = pltpu.make_async_copy(mod_hbm, mod_v, load_sem.at[3])
    load_stale.start()
    load_states.start()
    load_mod.start()
    loads = []
    for part in range(D // W_ROWS):
        rows = pl.ds(part * W_ROWS, W_ROWS)
        loads.append(
            pltpu.make_async_copy(weight_hbm.at[rows], weight_v.at[rows], weight_sem.at[part])
        )
        loads[-1].start()
    load_text.start()

    barrier = pltpu.get_barrier_semaphore()

    @pl.loop(1, BLK)
    def _(step):
        pl.semaphore_signal(
            barrier, inc=1, device_id=(sec, lax.rem(me + step, BLK)), device_id_type=MESH
        )

    @pl.loop(0, BLK)
    def _(step):
        pl.semaphore_signal(
            barrier, inc=1, device_id=(before, lax.rem(me + step, BLK)), device_id_type=MESH
        )

    core = lax.rem(me, 2)
    chip = me // 2
    sibling = me + 1 - 2 * core
    spare_index = me // SPARE_DEVICES
    has_spare = spare_index < SPARE_HEADS
    first_block = SPARE * lax.rem(me, SPARE_DEVICES)
    SPARE_CHIPS = SPARE_HEADS * SPARE_DEVICES // 2

    def remote(source, target, send, recv, to, section=None):
        return pltpu.make_async_remote_copy(
            src_ref=source,
            dst_ref=target,
            send_sem=send,
            recv_sem=recv,
            device_id=(sec if section is None else section, to),
            device_id_type=MESH,
        )

    def arrived(ref, sem):
        pltpu.make_async_copy(ref, ref, sem).wait()

    def send_main(kind):
        @pl.loop(1, BLK)
        def _(step):
            to = lax.rem(me + step, BLK)
            remote(
                main_send.at[kind, to],
                main_recv.at[kind, me],
                main_ssem.at[kind],
                main_rsem.at[kind],
                to,
            ).start()

        pltpu.make_async_copy(
            main_send.at[kind, me], main_recv.at[kind, me], main_rsem.at[kind]
        ).start()

    def spare_copy(kind, to_chip):
        return remote(
            spare_send.at[kind, 2 * to_chip // SPARE_DEVICES],
            spare_recv.at[kind, 8 * core + chip],
            spare_ssem.at[kind, to_chip],
            spare_rsem.at[kind],
            2 * to_chip + core,
        )

    def send_spare(kind):
        @pl.loop(0, BLK // 2)
        def _(step):
            to_chip = lax.rem(chip + step, BLK // 2)

            @pl.when(jnp.logical_and(to_chip != chip, to_chip < SPARE_CHIPS))
            def _():
                spare_copy(kind, to_chip).start()

        @pl.when(has_spare)
        def _():
            pltpu.make_async_copy(
                spare_send.at[kind, spare_index],
                spare_recv.at[kind, 8 * core + chip],
                spare_rsem.at[kind],
            ).start()

    def pass_copy(kind):
        block = spare_recv.at[kind, pl.ds(8 * core, 8)]
        return remote(block, block, pass_ssem.at[kind], pass_rsem.at[kind], sibling)

    def pass_spare(kind):
        @pl.when(has_spare)
        def _():
            arrived(spare_recv.at[kind, pl.ds(8 * core, 8)], spare_rsem.at[kind])
            pass_copy(kind).start()

    load_stale.wait()
    first_worked = patch_ref[0] == 0
    for index in range(HEADS):
        cols = slice(128 * index, 128 * index + 128)
        entries_v[:, cols] = jnp.where(first_worked, stale_v[1, :, cols], stale_v[0, :, cols])
    pack_heads(entries_v, main_send.at[0], spare_send.at[0])
    pl.semaphore_wait(barrier, 2 * BLK - 1)
    send_main(0)

    load_states.wait()
    load_mod.wait()
    row = step_ref[0]
    normed = (
        layer_norm(states_v[...].astype(F32).T) * (1.0 + mod_v[row, 1]) + mod_v[row, 0]
    ).astype(BF)
    for load in loads:
        load.wait()

    block_ones = (
        (lax.broadcasted_iota(jnp.int32, (128, 128), 0) < HD)
        == (lax.broadcasted_iota(jnp.int32, (128, 128), 1) < HD)
    ).astype(BF)
    query_gain = query_gain_ref[...]
    key_gain = key_gain_ref[...]

    def project(first, last):
        proj_v[:, first:last] = jnp.dot(
            normed, weight_v[:, first:last], preferred_element_type=F32
        )

    def normed_tile(index):
        value = proj_v[:, 128 * index : 128 * index + 128]
        square = value * value
        high = square.astype(BF)
        low = (square - high.astype(F32)).astype(BF)
        mean = (
            jnp.dot(high, block_ones, preferred_element_type=F32)
            + jnp.dot(low, block_ones, preferred_element_type=F32)
        ) * (1.0 / HD)
        gain = jnp.concatenate(
            [
                query_gain if index < 10 else key_gain,
                query_gain if index < 9 else key_gain,
            ],
            axis=1,
        )
        return value * lax.rsqrt(mean + 1e-06) * gain

    low64 = low_half(HD)
    project(0, 1280)
    for index in range(10):
        value = normed_tile(index)
        if index == 9:
            proj_v[:, 128 * index : 128 * index + 128] = value
        top, bottom = value[:HD], value[HD:]
        even = jnp.where(low64, top, swap_halves(bottom))
        q_send[2 * index] = (even.astype(BF).astype(F32) * 0.125).astype(BF)
        if index < 9:
            odd = jnp.where(low64, swap_halves(top), bottom)
            q_send[2 * index + 1] = (odd.astype(BF).astype(F32) * 0.125).astype(BF)

    @pl.loop(1, BLK)
    def _(step):
        to = lax.rem(me + step, BLK)
        remote(q_send.at[to], q_recv.at[me], q_ssem, q_rsem, to).start()

    pltpu.make_async_copy(q_send.at[me], q_recv.at[me], q_rsem).start()

    slot_there = lax.rem(me, SPARE)

    def spare_target(index):
        return SPARE_DEVICES * index + me // SPARE

    def query_copy(index):
        return remote(
            q_send.at[BLK + index],
            q_spare.at[slot_there],
            q_ssem2.at[index],
            q_rsem2.at[slot_there],
            spare_target(index),
        )

    def state_rows(head):
        return states_v.at[pl.ds(pl.multiple_of(HD * head, HD), HD)]

    def state_copy(index):
        return remote(
            state_rows(BLK + index),
            state_spare.at[slot_there],
            state_ssem2.at[index],
            state_rsem2.at[slot_there],
            spare_target(index),
        )

    for index in range(SPARE_HEADS):

        @pl.when(spare_target(index) != me)
        def _():
            query_copy(index).start()

        @pl.when(spare_target(index) == me)
        def _():
            pltpu.make_async_copy(
                q_send.at[BLK + index], q_spare.at[slot_there], q_rsem2.at[slot_there]
            ).start()

    project(1280, 2432)
    project(2432, 3648)
    low = low_half(TOK)

    def swapped_tile(index):
        if index == 9 or index >= 19:
            return swap_halves(proj_v[:, 128 * index : 128 * index + 128])
        return swap_halves(normed_tile(index))

    left = swapped_tile(9)
    for index in range(HEADS):
        right = swapped_tile(10 + index)
        fresh_v[:, 128 * index : 128 * index + 128] = jnp.where(low, left, right).astype(BF)
        left = right
    fresh_copy = pltpu.make_async_copy(fresh_v, fresh_hbm, fresh_sem)
    fresh_copy.start()
    pack_heads(fresh_v, main_send.at[1], spare_send.at[1])
    send_main(1)

    @pl.loop(1, BLK)
    def _(step):
        to = lax.rem(me + step, BLK)
        remote(state_rows(to), state_recv.at[me], state_ssem, state_rsem, to).start()

    pltpu.make_async_copy(state_rows(me), state_recv.at[me], state_rsem).start()
    for index in range(SPARE_HEADS):

        @pl.when(spare_target(index) != me)
        def _():
            state_copy(index).start()

        @pl.when(spare_target(index) == me)
        def _():
            pltpu.make_async_copy(
                state_rows(BLK + index), state_spare.at[slot_there], state_rsem2.at[slot_there]
            ).start()

    send_spare(0)
    send_spare(1)

    load_text.wait()
    text_normed = (
        layer_norm(text_v[...].astype(F32).T) * (1.0 + mod_v[row, 4]) + mod_v[row, 3]
    ).astype(BF)
    text_send[...] = (
        lax.dot_general(
            text_weight_ref[...],
            text_normed,
            (((1,), (1,)), ((), ())),
            preferred_element_type=F32,
        )
        .astype(BF)
        .astype(F32)
    )

    def text_main(step):
        unit = TEXT_COLS // 8 * me + step
        second = unit // TEXT_COLS
        head = (unit - TEXT_COLS * second) // 8
        to_row = pl.multiple_of(HD * second + 8 * lax.rem(unit, 8), 8)
        source = text_send.at[pl.ds(pl.multiple_of(8 * step, 8), 8)]
        target = text_recv.at[0, pl.ds(to_row, 8)]
        return (
            head,
            lambda: remote(source, target, text_ssem.at[step], text_rsem.at[0], head),
            lambda: pltpu.make_async_copy(source, target, text_rsem.at[0]),
        )

    @pl.loop(0, TEXT_COLS // 8)
    def _(step):
        head, away, local = text_main(step)

        @pl.when(jnp.logical_and(head < BLK, head != me))
        def _():
            away().start()

        @pl.when(head == me)
        def _():
            local().start()

    pieces = ((6, 112, 40, 0, 0), (7, 0, 24, 0, 40), (7, 24, 64, 1, 0), (7, 88, 64, 2, 0))
    second_half = me // 8

    def text_spare(number, step):
        _, row, rows, index, to_row = pieces[number]
        to = SPARE_DEVICES * index + step
        source = text_send.at[pl.ds(row, rows)]
        target = text_recv.at[1, pl.ds(pl.multiple_of(HD * second_half + to_row, 8), rows)]
        return (
            to,
            lambda: remote(source, target, text_ssem2.at[number, step], text_rsem.at[1], to),
            lambda: pltpu.make_async_copy(source, target, text_rsem.at[1]),
        )

    for number in range(4):

        @pl.when(lax.rem(me, 8) == pieces[number][0])
        def _():
            @pl.loop(0, SPARE_DEVICES)
            def _(step):
                to, away, local = text_spare(number, step)

                @pl.when(to != me)
                def _():
                    away().start()

                @pl.when(to == me)
                def _():
                    local().start()

    one = jnp.ones((1, 128), F32)
    low1 = low_half(1)
    gate_pad = jnp.concatenate([mod_v[row, 2], jnp.zeros((1, 64), F32)], axis=1)
    for head in range(HEADS):
        gate = gate_pad[:, 128 * (head // 2) : 128 * (head // 2) + 128]
        if head % 2 == 0:
            gate = swap_halves(jnp.broadcast_to(gate, (8, 128)))[0:1]
        gate_v[head : head + 1, :] = jnp.where(low1, one, gate)

    arrived(q_recv, q_rsem)

    def spread_queries(packed, row):
        value = packed.astype(F32)
        zero = jnp.zeros_like(value)
        q_all[pl.ds(row, HD)] = jnp.where(low64, value, zero).astype(BF)
        q_all[pl.ds(row + HD, HD)] = jnp.where(low64, swap_halves(value), zero).astype(BF)

    @pl.loop(0, BLK)
    def _(step):
        spread_queries(q_recv[step], pl.multiple_of(step * TOK, TOK))

    @pl.when(has_spare)
    def _():
        for slot in range(SPARE):
            arrived(q_spare.at[slot], q_rsem2.at[slot])
            spread_queries(q_spare[slot], ROWS + slot * TOK)

    def with_ones(entries):
        return jnp.where(
            low_half(entries.shape[0]), jnp.ones(entries.shape, F32), entries.astype(F32)
        ).astype(BF)

    def attend(rows, entries, values):
        scores = lax.dot_general(
            q_all[rows], entries, (((1,), (1,)), ((), ())), preferred_element_type=F32
        )
        powers = jnp.exp(scores).astype(BF)
        return jnp.dot(powers, values, preferred_element_type=F32)

    def query_rows(step):
        return pl.ds(pl.multiple_of(step * QT, QT), QT)

    arrived(main_recv.at[0, pl.ds(0, BLK)], main_rsem.at[0])
    stale_entries = main_recv[0, 0:BLK].reshape(BLK * TOK, 128)
    stale_values = with_ones(stale_entries)

    @pl.loop(0, ROWS // QT)
    def _(step):
        acc[query_rows(step)] = attend(query_rows(step), stale_entries, stale_values)

    low256 = low_half(TEXT)
    text_gain = jnp.concatenate([text_gain_ref[...], jnp.ones((1, HD), F32)], axis=1)

    def text_entries(which):
        arrived(text_recv.at[which], text_rsem.at[which])
        value = text_recv[which].T
        square = jnp.where(low256, value * value, 0.0)
        mean = jnp.sum(square, axis=1, keepdims=True) * (1.0 / HD)
        scaled = value * lax.rsqrt(mean + 1e-06) * text_gain
        return jnp.where(low256, scaled, value).astype(BF).reshape(2, TOK, 128)

    main_recv[1, BLK : BLK + 2] = text_entries(0)
    arrived(main_recv.at[1, pl.ds(0, BLK)], main_rsem.at[1])
    fresh_entries = main_recv[1].reshape((BLK + 2) * TOK, 128)
    fresh_values = with_ones(fresh_entries)

    def result_of(row, head, states):
        value = acc[pl.ds(row, TOK)] * gate_v[pl.ds(head, 1), :]
        turned = value.T
        return (states.astype(F32) + turned[HD:] / turned[:HD]).astype(BF)

    def result_copy(slot, head, block, sem):
        target = out_hbm.at[pl.ds(pl.multiple_of(HD * head, HD), HD)]
        return remote(out_send.at[slot], target, sem, out_rsem, block, after)

    def finish(step):
        acc[query_rows(step)] += attend(query_rows(step), fresh_entries, fresh_values)
        for part in range(QT // TOK):
            block = step * (QT // TOK) + part
            out_send[block] = result_of(
                pl.multiple_of(block * TOK, TOK), me, state_recv[block]
            )
            result_copy(block, me, block, out_ssem).start()

    arrived(state_recv, state_rsem)
    pass_spare(0)
    finish(0)
    pass_spare(1)
    pl.loop(1, ROWS // QT)(finish)

    @pl.when(has_spare)
    def _():
        spare_recv[1, BLK : BLK + 2] = text_entries(1)
        for kind in range(2):
            arrived(spare_recv.at[kind, pl.ds(8 * (1 - core), 8)], pass_rsem.at[kind])
            pass_copy(kind).wait_send()
        rows = pl.ds(ROWS, SPARE_ROWS)
        total = jnp.zeros((SPARE_ROWS, 128), F32)
        for kind, tiles in ((0, BLK), (1, BLK + 2)):
            entries = spare_recv[kind, 0:tiles].reshape(tiles * TOK, 128)
            total = total + attend(rows, entries, with_ones(entries))
        acc[rows] = total
        for slot in range(SPARE):
            arrived(state_spare.at[slot], state_rsem2.at[slot])
            out_send[BLK + slot] = result_of(
                ROWS + slot * TOK, BLK + spare_index, state_spare[slot]
            )
            result_copy(
                BLK + slot, BLK + spare_index, first_block + slot, out_ssem2.at[slot]
            ).start()

    arrived(out_hbm, out_rsem)

    fresh_copy.wait()
    for kind in range(2):
        arrived(main_send.at[kind, pl.ds(0, BLK - 1)], main_ssem.at[kind])

        @pl.loop(0, SPARE_CHIPS)
        def _(to_chip):
            @pl.when(to_chip != chip)
            def _():
                spare_copy(kind, to_chip).wait_send()

    arrived(q_send.at[pl.ds(0, BLK - 1)], q_ssem)
    arrived(state_recv.at[pl.ds(0, BLK - 1)], state_ssem)
    for index in range(SPARE_HEADS):

        @pl.when(spare_target(index) != me)
        def _():
            query_copy(index).wait_send()
            state_copy(index).wait_send()

    @pl.loop(0, TEXT_COLS // 8)
    def _(step):
        head, away, _ = text_main(step)

        @pl.when(jnp.logical_and(head < BLK, head != me))
        def _():
            away().wait_send()

    for number in range(4):

        @pl.when(lax.rem(me, 8) == pieces[number][0])
        def _():
            @pl.loop(0, SPARE_DEVICES)
            def _(step):
                to, away, _ = text_spare(number, step)

                @pl.when(to != me)
                def _():
                    away().wait_send()

    arrived(out_send.at[pl.ds(0, BLK)], out_ssem)

    @pl.when(has_spare)
    def _():
        for slot in range(SPARE):
            result_copy(
                BLK + slot, BLK + spare_index, first_block + slot, out_ssem2.at[slot]
            ).wait_send()


def write_results(raw_states, raw_fresh, states_out, fresh_out, sems):
    copies = (
        pltpu.make_async_copy(raw_states, states_out, sems.at[0]),
        pltpu.make_async_copy(raw_fresh, fresh_out, sems.at[1]),
    )
    for copy in copies:
        copy.start()
    for copy in copies:
        copy.wait()


def body(
    sections,
    states,
    image_weight,
    text_weight,
    text_states,
    stale_cache,
    modulation,
    query_gain,
    key_gain,
    text_gain,
    timestep,
    layer_patch_index,
):
    vmem = pl.BlockSpec(memory_space=pltpu.VMEM)
    anywhere = pl.BlockSpec(memory_space=pl.ANY)
    dma = pltpu.SemaphoreType.DMA
    next_states, fresh = pl.pallas_call(
        functools.partial(kernel, sections),
        out_shape=(
            jax.ShapeDtypeStruct((D, TOK), BF),
            jax.ShapeDtypeStruct((TOK, 2 * D), BF),
        ),
        in_specs=[
            pl.BlockSpec(memory_space=pltpu.SMEM),
            pl.BlockSpec(memory_space=pltpu.SMEM),
            anywhere,
            anywhere,
            vmem,
            anywhere,
            anywhere,
            anywhere,
            vmem,
            vmem,
            vmem,
        ],
        out_specs=(anywhere, anywhere),
        scratch_shapes=[
            pltpu.VMEM((D, TOK), BF),
            pltpu.VMEM((D, 3 * D), BF),
            pltpu.VMEM((D, TEXT), BF),
            pltpu.VMEM((2, TOK, 2 * D), BF),
            pltpu.VMEM((modulation.shape[0], 5, 1, D), F32),
            pltpu.VMEM((TOK, 2 * D), BF),
            pltpu.VMEM((TOK, 3 * D + 64), F32),
            pltpu.VMEM((TOK, 2 * D), BF),
            pltpu.VMEM((2, BLK, TOK, 128), BF),
            pltpu.VMEM((2, BLK + 2, TOK, 128), BF),
            pltpu.VMEM((2, SPARE_HEADS, TOK, 128), BF),
            pltpu.VMEM((2, BLK + 2, TOK, 128), BF),
            pltpu.VMEM((HEADS, HD, 128), BF),
            pltpu.VMEM((BLK, HD, 128), BF),
            pltpu.VMEM((SPARE, HD, 128), BF),
            pltpu.VMEM((ROWS + SPARE_ROWS, 128), BF),
            pltpu.VMEM((BLK, HD, 128), BF),
            pltpu.VMEM((SPARE, HD, 128), BF),
            pltpu.VMEM((ROWS + SPARE_ROWS, 128), F32),
            pltpu.VMEM((TEXT_COLS, TEXT), F32),
            pltpu.VMEM((2, 128, TEXT), F32),
            pltpu.VMEM((24, 128), F32),
            pltpu.VMEM((BLK + SPARE, HD, 128), BF),
            dma((4,)),
            dma((D // W_ROWS,)),
            dma((2,)),
            dma((2,)),
            dma((2, BLK // 2)),
            dma((2,)),
            dma((2,)),
            dma((2,)),
            dma,
            dma,
            dma((SPARE_HEADS,)),
            dma((SPARE,)),
            dma,
            dma,
            dma((SPARE_HEADS,)),
            dma((SPARE,)),
            dma((TEXT_COLS // 8,)),
            dma((4, SPARE_DEVICES)),
            dma((2,)),
            dma,
            dma((SPARE,)),
            dma,
            dma,
        ],
        compiler_params=pltpu.CompilerParams(
            collective_id=0, has_side_effects=True, vmem_limit_bytes=56 * 1024 * 1024
        ),
    )(
        layer_patch_index,
        timestep,
        jnp.swapaxes(states[0], 0, 1),
        image_weight[0],
        jnp.swapaxes(text_weight[0], 0, 1),
        jnp.swapaxes(text_states[0], 0, 1),
        stale_cache[0],
        jnp.swapaxes(modulation, 1, 2),
        query_gain,
        key_gain,
        text_gain,
    )
    next_states, fresh = pl.pallas_call(
        write_results,
        out_shape=(
            jax.ShapeDtypeStruct((D, TOK), BF),
            jax.ShapeDtypeStruct((TOK, 2 * D), BF),
        ),
        in_specs=[anywhere, anywhere],
        out_specs=(anywhere, anywhere),
        scratch_shapes=[dma((2,))],
        compiler_params=pltpu.CompilerParams(vmem_limit_bytes=60 * 1024 * 1024),
    )(next_states, fresh)
    return (jnp.swapaxes(next_states, 0, 1)[None], fresh[None])


def solution(mesh):
    in_specs = (
        P("section", "blk", None),
        P("section", None, None),
        P("section", None, "blk"),
        P("section", None, None),
        P("section", None, "blk", None),
        P(None, "section", None, None),
        P("section", None),
        P("section", None),
        P("section", None),
        P("section"),
        P("section"),
    )
    out_specs = (P("section", "blk", None), P("section", "blk", None))
    return jax.shard_map(
        functools.partial(body, mesh.shape["section"]),
        mesh=mesh,
        in_specs=in_specs,
        out_specs=out_specs,
        check_vma=False,
    )
```

```python
import functools

import jax
import jax.numpy as jnp
from jax import lax
from jax.experimental import pallas as pl
from jax.experimental.pallas import tpu as pltpu
from jax.sharding import PartitionSpec as P

MESH = pl.DeviceIdType.MESH
BF = jnp.bfloat16
F32 = jnp.float32

D = 1216
HEADS = 19
HD = 64
TOK = 128
TEXT = 256
BLK = 16
TEXT_COLS = 152
SPARE = 4
ROWS = BLK * TOK
SPARE_ROWS = SPARE * TOK
W_ROWS = 304
SPARE_DEVICES = 4
SPARE_HEADS = 3
QT = 512


def low_half(rows):
    return lax.broadcasted_iota(jnp.int32, (rows, 128), 1) < HD


def swap_halves(value):
    return pltpu.roll(value, HD, axis=1)


def layer_norm(values):
    center = values - jnp.mean(values, axis=-1, keepdims=True)
    return center * lax.rsqrt(jnp.mean(center * center, axis=-1, keepdims=True) + 1e-06)


def pack_heads(source, mains, spares):
    low = low_half(TOK)

    def tile(index):
        return source[:, 128 * index : 128 * index + 128].astype(F32)

    for head in range(HEADS):
        half = head // 2
        if head % 2 == 0:
            packed = jnp.where(low, tile(half), tile(9 + half))
        else:
            packed = swap_halves(jnp.where(low, tile(10 + half), tile(half)))
        if head < BLK:
            mains[head] = packed.astype(BF)
        else:
            spares[head - BLK] = packed.astype(BF)


def kernel(
    sections,
    patch_ref,
    step_ref,
    states_hbm,
    weight_hbm,
    text_weight_ref,
    text_hbm,
    stale_hbm,
    mod_hbm,
    query_gain_ref,
    key_gain_ref,
    text_gain_ref,
    out_hbm,
    fresh_hbm,
    states_v,
    weight_v,
    text_v,
    stale_v,
    mod_v,
    entries_v,
    proj_v,
    fresh_v,
    main_send,
    main_recv,
    spare_send,
    spare_recv,
    q_send,
    q_recv,
    q_spare,
    q_all,
    state_recv,
    state_spare,
    acc,
    text_send,
    text_recv,
    gate_v,
    out_send,
    load_sem,
    weight_sem,
    main_ssem,
    main_rsem,
    spare_ssem,
    spare_rsem,
    pass_ssem,
    pass_rsem,
    q_ssem,
    q_rsem,
    q_ssem2,
    q_rsem2,
    state_ssem,
    state_rsem,
    state_ssem2,
    state_rsem2,
    text_ssem,
    text_ssem2,
    text_rsem,
    out_ssem,
    out_ssem2,
    out_rsem,
    fresh_sem,
):
    sec = lax.axis_index("section")
    me = lax.axis_index("blk")
    after = lax.rem(sec + 1, sections)
    before = lax.rem(sec + sections - 1, sections)

    load_stale = pltpu.make_async_copy(stale_hbm, stale_v, load_sem.at[0])
    load_states = pltpu.make_async_copy(states_hbm, states_v, load_sem.at[1])
    load_text = pltpu.make_async_copy(text_hbm, text_v, load_sem.at[2])
    load_mod = pltpu.make_async_copy(mod_hbm, mod_v, load_sem.at[3])
    load_stale.start()
    load_states.start()
    load_mod.start()
    load_text.start()
    loads = []
    for part in range(D // W_ROWS):
        rows = pl.ds(part * W_ROWS, W_ROWS)
        loads.append(
            pltpu.make_async_copy(weight_hbm.at[rows], weight_v.at[rows], weight_sem.at[part])
        )
        loads[-1].start()

    barrier = pltpu.get_barrier_semaphore()

    @pl.loop(1, BLK)
    def _(step):
        pl.semaphore_signal(
            barrier, inc=1, device_id=(sec, lax.rem(me + step, BLK)), device_id_type=MESH
        )

    @pl.loop(0, BLK)
    def _(step):
        pl.semaphore_signal(
            barrier, inc=1, device_id=(before, lax.rem(me + step, BLK)), device_id_type=MESH
        )

    core = lax.rem(me, 2)
    chip = me // 2
    sibling = me + 1 - 2 * core
    spare_index = me // SPARE_DEVICES
    has_spare = spare_index < SPARE_HEADS
    first_block = SPARE * lax.rem(me, SPARE_DEVICES)
    SPARE_CHIPS = SPARE_HEADS * SPARE_DEVICES // 2

    def peer(step):
        ring = step // 4
        up = jnp.where(ring == 0, 2, jnp.where(ring == 1, 1, jnp.where(ring == 2, 3, 0)))
        rest = lax.rem(step, 4)
        to_x = lax.rem(me // 8 + 1 - rest // 2, 2)
        to_y = lax.rem(chip + up, 4)
        to_core = lax.rem(core + 1 - lax.rem(rest, 2), 2)
        return 8 * to_x + 2 * to_y + to_core

    def remote(source, target, send, recv, to, section=None):
        return pltpu.make_async_remote_copy(
            src_ref=source,
            dst_ref=target,
            send_sem=send,
            recv_sem=recv,
            device_id=(sec if section is None else section, to),
            device_id_type=MESH,
        )

    def arrived(ref, sem):
        pltpu.make_async_copy(ref, ref, sem).wait()

    def send_main(kind):
        @pl.loop(0, BLK - 1)
        def _(step):
            to = peer(step)
            remote(
                main_send.at[kind, to],
                main_recv.at[kind, me],
                main_ssem.at[kind],
                main_rsem.at[kind],
                to,
            ).start()

        pltpu.make_async_copy(
            main_send.at[kind, me], main_recv.at[kind, me], main_rsem.at[kind]
        ).start()

    def spare_copy(kind, to_chip):
        return remote(
            spare_send.at[kind, 2 * to_chip // SPARE_DEVICES],
            spare_recv.at[kind, 8 * core + chip],
            spare_ssem.at[kind, to_chip],
            spare_rsem.at[kind],
            2 * to_chip + core,
        )

    def send_spare(kind):
        @pl.loop(0, BLK // 2)
        def _(step):
            to_chip = peer(2 * step) // 2

            @pl.when(jnp.logical_and(to_chip != chip, to_chip < SPARE_CHIPS))
            def _():
                spare_copy(kind, to_chip).start()

        @pl.when(has_spare)
        def _():
            pltpu.make_async_copy(
                spare_send.at[kind, spare_index],
                spare_recv.at[kind, 8 * core + chip],
                spare_rsem.at[kind],
            ).start()

    def pass_copy(kind):
        block = spare_recv.at[kind, pl.ds(8 * core, 8)]
        return remote(block, block, pass_ssem.at[kind], pass_rsem.at[kind], sibling)

    def pass_spare(kind):
        @pl.when(has_spare)
        def _():
            arrived(spare_recv.at[kind, pl.ds(8 * core, 8)], spare_rsem.at[kind])
            pass_copy(kind).start()

    load_stale.wait()
    first_worked = patch_ref[0] == 0
    for index in range(HEADS):
        cols = slice(128 * index, 128 * index + 128)
        entries_v[:, cols] = jnp.where(first_worked, stale_v[1, :, cols], stale_v[0, :, cols])
    pack_heads(entries_v, main_send.at[0], spare_send.at[0])
    pl.semaphore_wait(barrier, 2 * BLK - 1)
    send_main(0)

    load_text.wait()
    load_mod.wait()
    row = step_ref[0]
    text_normed = (
        layer_norm(text_v[...].astype(F32).T) * (1.0 + mod_v[row, 4]) + mod_v[row, 3]
    ).astype(BF)
    text_part = lax.dot_general(
        text_weight_ref[...],
        text_normed,
        (((1,), (1,)), ((), ())),
        preferred_element_type=F32,
    )
    for unit in range(TEXT_COLS // 8):
        eight = text_part[8 * unit : 8 * unit + 8]
        text_send[unit] = jnp.concatenate([eight[:, :128], eight[:, 128:]], axis=0).astype(BF)

    def text_main(step):
        unit = TEXT_COLS // 8 * me + step
        second = unit // TEXT_COLS
        head = (unit - TEXT_COLS * second) // 8
        source = text_send.at[step]
        target = text_recv.at[0, 8 * second + lax.rem(unit, 8)]
        return (
            head,
            lambda: remote(source, target, text_ssem.at[step], text_rsem.at[0], head),
            lambda: pltpu.make_async_copy(source, target, text_rsem.at[0]),
        )

    @pl.loop(0, TEXT_COLS // 8)
    def _(step):
        head, away, local = text_main(step)

        @pl.when(jnp.logical_and(head < BLK, head != me))
        def _():
            away().start()

        @pl.when(head == me)
        def _():
            local().start()

    pieces = ((6, 14, 5, 0, 0), (7, 0, 3, 0, 5), (7, 3, 8, 1, 0), (7, 11, 8, 2, 0))
    second_half = me // 8

    def text_spare(number, step):
        _, row, rows, index, to_row = pieces[number]
        to = SPARE_DEVICES * index + step
        source = text_send.at[pl.ds(row, rows)]
        target = text_recv.at[1, pl.ds(8 * second_half + to_row, rows)]
        return (
            to,
            lambda: remote(source, target, text_ssem2.at[number, step], text_rsem.at[1], to),
            lambda: pltpu.make_async_copy(source, target, text_rsem.at[1]),
        )

    for number in range(4):

        @pl.when(lax.rem(me, 8) == pieces[number][0])
        def _():
            @pl.loop(0, SPARE_DEVICES)
            def _(step):
                to, away, local = text_spare(number, step)

                @pl.when(to != me)
                def _():
                    away().start()

                @pl.when(to == me)
                def _():
                    local().start()

    slot_there = lax.rem(me, SPARE)

    def spare_target(index):
        return SPARE_DEVICES * index + me // SPARE

    def query_copy(index):
        return remote(
            q_send.at[BLK + index],
            q_spare.at[slot_there],
            q_ssem2.at[index],
            q_rsem2.at[slot_there],
            spare_target(index),
        )

    def state_rows(head):
        return states_v.at[pl.ds(pl.multiple_of(HD * head, HD), HD)]

    def state_copy(index):
        return remote(
            state_rows(BLK + index),
            state_spare.at[slot_there],
            state_ssem2.at[index],
            state_rsem2.at[slot_there],
            spare_target(index),
        )

    load_states.wait()
    normed = (
        layer_norm(states_v[...].astype(F32).T) * (1.0 + mod_v[row, 1]) + mod_v[row, 0]
    ).astype(BF)
    for load in loads:
        load.wait()

    block_ones = (
        (lax.broadcasted_iota(jnp.int32, (128, 128), 0) < HD)
        == (lax.broadcasted_iota(jnp.int32, (128, 128), 1) < HD)
    ).astype(BF)
    query_gain = query_gain_ref[...]
    key_gain = key_gain_ref[...]

    def project(first, last):
        proj_v[:, first:last] = jnp.dot(
            normed, weight_v[:, first:last], preferred_element_type=F32
        )

    def normed_tile(index):
        value = proj_v[:, 128 * index : 128 * index + 128]
        square = value * value
        high = square.astype(BF)
        low = (square - high.astype(F32)).astype(BF)
        mean = (
            jnp.dot(high, block_ones, preferred_element_type=F32)
            + jnp.dot(low, block_ones, preferred_element_type=F32)
        ) * (1.0 / HD)
        gain = jnp.concatenate(
            [
                query_gain if index < 10 else key_gain,
                query_gain if index < 9 else key_gain,
            ],
            axis=1,
        )
        return value * lax.rsqrt(mean + 1e-06) * gain

    low64 = low_half(HD)
    project(0, 1280)
    for index in range(10):
        value = normed_tile(index)
        if index == 9:
            proj_v[:, 128 * index : 128 * index + 128] = value
        top, bottom = value[:HD], value[HD:]
        even = jnp.where(low64, top, swap_halves(bottom))
        q_send[2 * index] = (even.astype(BF).astype(F32) * 0.125).astype(BF)
        if index < 9:
            odd = jnp.where(low64, swap_halves(top), bottom)
            q_send[2 * index + 1] = (odd.astype(BF).astype(F32) * 0.125).astype(BF)

    @pl.loop(0, BLK - 1)
    def _(step):
        to = peer(step)
        remote(q_send.at[to], q_recv.at[me], q_ssem, q_rsem, to).start()

    pltpu.make_async_copy(q_send.at[me], q_recv.at[me], q_rsem).start()

    for index in range(SPARE_HEADS):

        @pl.when(spare_target(index) != me)
        def _():
            query_copy(index).start()

        @pl.when(spare_target(index) == me)
        def _():
            pltpu.make_async_copy(
                q_send.at[BLK + index], q_spare.at[slot_there], q_rsem2.at[slot_there]
            ).start()

    @pl.loop(0, BLK - 1)
    def _(step):
        to = peer(step)
        remote(state_rows(to), state_recv.at[me], state_ssem, state_rsem, to).start()

    pltpu.make_async_copy(state_rows(me), state_recv.at[me], state_rsem).start()
    for index in range(SPARE_HEADS):

        @pl.when(spare_target(index) != me)
        def _():
            state_copy(index).start()

        @pl.when(spare_target(index) == me)
        def _():
            pltpu.make_async_copy(
                state_rows(BLK + index), state_spare.at[slot_there], state_rsem2.at[slot_there]
            ).start()

    project(1280, 2432)
    project(2432, 3648)
    low = low_half(TOK)

    def swapped_tile(index):
        if index == 9 or index >= 19:
            return swap_halves(proj_v[:, 128 * index : 128 * index + 128])
        return swap_halves(normed_tile(index))

    left = swapped_tile(9)
    for index in range(HEADS):
        right = swapped_tile(10 + index)
        fresh_v[:, 128 * index : 128 * index + 128] = jnp.where(low, left, right).astype(BF)
        left = right
    fresh_copy = pltpu.make_async_copy(fresh_v, fresh_hbm, fresh_sem)
    fresh_copy.start()
    pack_heads(fresh_v, main_send.at[1], spare_send.at[1])
    send_main(1)

    send_spare(0)
    send_spare(1)

    one = jnp.ones((1, 128), F32)
    low1 = low_half(1)
    gate_pad = jnp.concatenate([mod_v[row, 2], jnp.zeros((1, 64), F32)], axis=1)
    for head in range(HEADS):
        gate = gate_pad[:, 128 * (head // 2) : 128 * (head // 2) + 128]
        if head % 2 == 0:
            gate = swap_halves(jnp.broadcast_to(gate, (8, 128)))[0:1]
        gate_v[head : head + 1, :] = jnp.where(low1, one, gate)

    arrived(q_recv, q_rsem)

    def spread_queries(packed, row):
        value = packed.astype(F32)
        zero = jnp.zeros_like(value)
        q_all[pl.ds(row, HD)] = jnp.where(low64, value, zero).astype(BF)
        q_all[pl.ds(row + HD, HD)] = jnp.where(low64, swap_halves(value), zero).astype(BF)

    @pl.loop(0, BLK)
    def _(step):
        spread_queries(q_recv[step], pl.multiple_of(step * TOK, TOK))

    @pl.when(has_spare)
    def _():
        for slot in range(SPARE):
            arrived(q_spare.at[slot], q_rsem2.at[slot])
            spread_queries(q_spare[slot], ROWS + slot * TOK)

    def with_ones(entries):
        return jnp.where(
            low_half(entries.shape[0]), jnp.ones(entries.shape, F32), entries.astype(F32)
        ).astype(BF)

    def attend(rows, entries, values):
        scores = lax.dot_general(
            q_all[rows], entries, (((1,), (1,)), ((), ())), preferred_element_type=F32
        )
        powers = jnp.exp(scores).astype(BF)
        return jnp.dot(powers, values, preferred_element_type=F32)

    def query_rows(step):
        return pl.ds(pl.multiple_of(step * QT, QT), QT)

    arrived(main_recv.at[0, pl.ds(0, BLK)], main_rsem.at[0])
    stale_entries = main_recv[0, 0:BLK].reshape(BLK * TOK, 128)
    stale_values = with_ones(stale_entries)

    @pl.loop(0, ROWS // QT)
    def _(step):
        acc[query_rows(step)] = attend(query_rows(step), stale_entries, stale_values)

    low256 = low_half(TEXT)
    text_gain = jnp.concatenate([text_gain_ref[...], jnp.ones((1, HD), F32)], axis=1)

    def text_entries(which):
        arrived(text_recv.at[which], text_rsem.at[which])
        tiles = text_recv[which].astype(F32)
        halves = [tiles[:, 8 * half : 8 * half + 8].reshape(128, 128) for half in range(2)]
        value = jnp.concatenate([halves[0].T, halves[1].T], axis=0)
        square = jnp.where(low256, value * value, 0.0)
        mean = jnp.sum(square, axis=1, keepdims=True) * (1.0 / HD)
        scaled = value * lax.rsqrt(mean + 1e-06) * text_gain
        return jnp.where(low256, scaled, value).astype(BF).reshape(2, TOK, 128)

    main_recv[1, BLK : BLK + 2] = text_entries(0)
    arrived(main_recv.at[1, pl.ds(0, BLK)], main_rsem.at[1])
    fresh_entries = main_recv[1].reshape((BLK + 2) * TOK, 128)
    fresh_values = with_ones(fresh_entries)

    def result_of(row, head, states):
        value = acc[pl.ds(row, TOK)] * gate_v[pl.ds(head, 1), :]
        turned = value.T
        return (states.astype(F32) + turned[HD:] / turned[:HD]).astype(BF)

    def result_copy(slot, head, block, sem):
        target = out_hbm.at[pl.ds(pl.multiple_of(HD * head, HD), HD)]
        return remote(out_send.at[slot], target, sem, out_rsem, block, after)

    def finish(turn):
        step = lax.rem(me + turn, ROWS // QT)
        acc[query_rows(step)] += attend(query_rows(step), fresh_entries, fresh_values)
        for part in range(QT // TOK):
            block = step * (QT // TOK) + part
            out_send[block] = result_of(
                pl.multiple_of(block * TOK, TOK), me, state_recv[block]
            )
            result_copy(block, me, block, out_ssem).start()

    arrived(state_recv, state_rsem)
    pl.loop(0, 2)(finish)
    pass_spare(0)
    pl.loop(2, ROWS // QT)(finish)
    pass_spare(1)

    @pl.when(has_spare)
    def _():
        spare_recv[1, BLK : BLK + 2] = text_entries(1)
        rows = pl.ds(ROWS, SPARE_ROWS)
        total = jnp.zeros((SPARE_ROWS, 128), F32)
        for kind, tiles in ((0, BLK), (1, BLK + 2)):
            arrived(spare_recv.at[kind, pl.ds(8 * (1 - core), 8)], pass_rsem.at[kind])
            entries = spare_recv[kind, 0:tiles].reshape(tiles * TOK, 128)
            total = total + attend(rows, entries, with_ones(entries))
        acc[rows] = total
        for slot in range(SPARE):
            arrived(state_spare.at[slot], state_rsem2.at[slot])
            out_send[BLK + slot] = result_of(
                ROWS + slot * TOK, BLK + spare_index, state_spare[slot]
            )
            result_copy(
                BLK + slot, BLK + spare_index, first_block + slot, out_ssem2.at[slot]
            ).start()

    arrived(out_hbm, out_rsem)

    fresh_copy.wait()
    for kind in range(2):
        arrived(main_send.at[kind, pl.ds(0, BLK - 1)], main_ssem.at[kind])

        @pl.loop(0, SPARE_CHIPS)
        def _(to_chip):
            @pl.when(to_chip != chip)
            def _():
                spare_copy(kind, to_chip).wait_send()

    arrived(q_send.at[pl.ds(0, BLK - 1)], q_ssem)
    arrived(state_recv.at[pl.ds(0, BLK - 1)], state_ssem)
    for index in range(SPARE_HEADS):

        @pl.when(spare_target(index) != me)
        def _():
            query_copy(index).wait_send()
            state_copy(index).wait_send()

    @pl.loop(0, TEXT_COLS // 8)
    def _(step):
        head, away, _ = text_main(step)

        @pl.when(jnp.logical_and(head < BLK, head != me))
        def _():
            away().wait_send()

    for number in range(4):

        @pl.when(lax.rem(me, 8) == pieces[number][0])
        def _():
            @pl.loop(0, SPARE_DEVICES)
            def _(step):
                to, away, _ = text_spare(number, step)

                @pl.when(to != me)
                def _():
                    away().wait_send()

    arrived(out_send.at[pl.ds(0, BLK)], out_ssem)

    @pl.when(has_spare)
    def _():
        for slot in range(SPARE):
            result_copy(
                BLK + slot, BLK + spare_index, first_block + slot, out_ssem2.at[slot]
            ).wait_send()
        for kind in range(2):
            pass_copy(kind).wait_send()


def write_results(raw_states, raw_fresh, states_out, fresh_out, states_v, fresh_v, sems):
    loads = (
        pltpu.make_async_copy(raw_fresh, fresh_v, sems.at[0]),
        pltpu.make_async_copy(raw_states, states_v, sems.at[1]),
    )
    stores = (
        pltpu.make_async_copy(fresh_v, fresh_out, sems.at[0]),
        pltpu.make_async_copy(states_v, states_out, sems.at[1]),
    )
    for load in loads:
        load.start()
    for load, store in zip(loads, stores):
        load.wait()
        store.start()
    for store in stores:
        store.wait()


def body(
    sections,
    states,
    image_weight,
    text_weight,
    text_states,
    stale_cache,
    modulation,
    query_gain,
    key_gain,
    text_gain,
    timestep,
    layer_patch_index,
):
    vmem = pl.BlockSpec(memory_space=pltpu.VMEM)
    anywhere = pl.BlockSpec(memory_space=pl.ANY)
    dma = pltpu.SemaphoreType.DMA
    next_states, fresh = pl.pallas_call(
        functools.partial(kernel, sections),
        out_shape=(
            jax.ShapeDtypeStruct((D, TOK), BF),
            jax.ShapeDtypeStruct((TOK, 2 * D), BF),
        ),
        in_specs=[
            pl.BlockSpec(memory_space=pltpu.SMEM),
            pl.BlockSpec(memory_space=pltpu.SMEM),
            anywhere,
            anywhere,
            vmem,
            anywhere,
            anywhere,
            anywhere,
            vmem,
            vmem,
            vmem,
        ],
        out_specs=(anywhere, anywhere),
        scratch_shapes=[
            pltpu.VMEM((D, TOK), BF),
            pltpu.VMEM((D, 3 * D), BF),
            pltpu.VMEM((D, TEXT), BF),
            pltpu.VMEM((2, TOK, 2 * D), BF),
            pltpu.VMEM((modulation.shape[0], 5, 1, D), F32),
            pltpu.VMEM((TOK, 2 * D), BF),
            pltpu.VMEM((TOK, 3 * D + 64), F32),
            pltpu.VMEM((TOK, 2 * D), BF),
            pltpu.VMEM((2, BLK, TOK, 128), BF),
            pltpu.VMEM((2, BLK + 2, TOK, 128), BF),
            pltpu.VMEM((2, SPARE_HEADS, TOK, 128), BF),
            pltpu.VMEM((2, BLK + 2, TOK, 128), BF),
            pltpu.VMEM((HEADS, HD, 128), BF),
            pltpu.VMEM((BLK, HD, 128), BF),
            pltpu.VMEM((SPARE, HD, 128), BF),
            pltpu.VMEM((ROWS + SPARE_ROWS, 128), BF),
            pltpu.VMEM((BLK, HD, 128), BF),
            pltpu.VMEM((SPARE, HD, 128), BF),
            pltpu.VMEM((ROWS + SPARE_ROWS, 128), F32),
            pltpu.VMEM((TEXT_COLS // 8, 16, 128), BF),
            pltpu.VMEM((2, 16, 16, 128), BF),
            pltpu.VMEM((24, 128), F32),
            pltpu.VMEM((BLK + SPARE, HD, 128), BF),
            dma((4,)),
            dma((D // W_ROWS,)),
            dma((2,)),
            dma((2,)),
            dma((2, BLK // 2)),
            dma((2,)),
            dma((2,)),
            dma((2,)),
            dma,
            dma,
            dma((SPARE_HEADS,)),
            dma((SPARE,)),
            dma,
            dma,
            dma((SPARE_HEADS,)),
            dma((SPARE,)),
            dma((TEXT_COLS // 8,)),
            dma((4, SPARE_DEVICES)),
            dma((2,)),
            dma,
            dma((SPARE,)),
            dma,
            dma,
        ],
        compiler_params=pltpu.CompilerParams(
            collective_id=0, has_side_effects=True, vmem_limit_bytes=56 * 1024 * 1024
        ),
    )(
        layer_patch_index,
        timestep,
        jnp.swapaxes(states[0], 0, 1),
        image_weight[0],
        jnp.swapaxes(text_weight[0], 0, 1),
        jnp.swapaxes(text_states[0], 0, 1),
        stale_cache[0],
        jnp.swapaxes(modulation, 1, 2),
        query_gain,
        key_gain,
        text_gain,
    )
    next_states, fresh = pl.pallas_call(
        write_results,
        out_shape=(
            jax.ShapeDtypeStruct((D, TOK), BF),
            jax.ShapeDtypeStruct((TOK, 2 * D), BF),
        ),
        in_specs=[anywhere, anywhere],
        out_specs=(anywhere, anywhere),
        scratch_shapes=[pltpu.VMEM((D, TOK), BF), pltpu.VMEM((TOK, 2 * D), BF), dma((2,))],
        compiler_params=pltpu.CompilerParams(vmem_limit_bytes=60 * 1024 * 1024),
    )(next_states, fresh)
    return (jnp.swapaxes(next_states, 0, 1)[None], fresh[None])


def solution(mesh):
    in_specs = (
        P("section", "blk", None),
        P("section", None, None),
        P("section", None, "blk"),
        P("section", None, None),
        P("section", None, "blk", None),
        P(None, "section", None, None),
        P("section", None),
        P("section", None),
        P("section", None),
        P("section"),
        P("section"),
    )
    out_specs = (P("section", "blk", None), P("section", "blk", None))
    return jax.shard_map(
        functools.partial(body, mesh.shape["section"]),
        mesh=mesh,
        in_specs=in_specs,
        out_specs=out_specs,
        check_vma=False,
    )
```

```python
import functools

import jax
import jax.numpy as jnp
from jax import lax
from jax.experimental import pallas as pl
from jax.experimental.pallas import tpu as pltpu
from jax.sharding import PartitionSpec as P

MESH = pl.DeviceIdType.MESH
BF = jnp.bfloat16
F32 = jnp.float32

D = 1216
HEADS = 19
HD = 64
TOK = 128
TEXT = 256
BLK = 16
TEXT_COLS = 152
SPARE = 4
ROWS = BLK * TOK
SPARE_ROWS = SPARE * TOK
W_ROWS = 304
SPARE_DEVICES = 4
SPARE_HEADS = 3
QT = 512


def low_half(rows):
    return lax.broadcasted_iota(jnp.int32, (rows, 128), 1) < HD


def swap_halves(value):
    return pltpu.roll(value, HD, axis=1)


def layer_norm(values):
    center = values - jnp.mean(values, axis=-1, keepdims=True)
    return center * lax.rsqrt(jnp.mean(center * center, axis=-1, keepdims=True) + 1e-06)


def pack_heads(source, mains, spares):
    low = low_half(TOK)

    def tile(index):
        return source[:, 128 * index : 128 * index + 128].astype(F32)

    for head in range(HEADS):
        half = head // 2
        if head % 2 == 0:
            packed = jnp.where(low, tile(half), tile(9 + half))
        else:
            packed = swap_halves(jnp.where(low, tile(10 + half), tile(half)))
        if head < BLK:
            mains[head] = packed.astype(BF)
        else:
            spares[head - BLK] = packed.astype(BF)


def kernel(
    sections,
    patch_ref,
    step_ref,
    states_hbm,
    weight_hbm,
    text_weight_ref,
    text_hbm,
    stale_hbm,
    mod_hbm,
    query_gain_ref,
    key_gain_ref,
    text_gain_ref,
    out_hbm,
    fresh_hbm,
    states_v,
    weight_v,
    text_v,
    stale_v,
    mod_v,
    entries_v,
    proj_v,
    fresh_v,
    main_send,
    kv,
    spare_send,
    q_send,
    q_recv,
    q_spare,
    q_all,
    state_recv,
    acc,
    text_send,
    text_recv,
    gate_v,
    out_send,
    load_sem,
    weight_sem,
    main_ssem,
    main_rsem,
    spare_ssem,
    spare_rsem,
    pass_ssem,
    pass_rsem,
    q_ssem,
    q_rsem,
    q_ssem2,
    q_rsem2,
    state_ssem,
    state_rsem,
    state_ssem2,
    state_rsem2,
    text_ssem,
    text_rsem,
    out_ssem,
    out_rsem,
    fresh_sem,
):
    sec = lax.axis_index("section")
    me = lax.axis_index("blk")
    after = lax.rem(sec + 1, sections)
    before = lax.rem(sec + sections - 1, sections)

    load_stale = pltpu.make_async_copy(stale_hbm, stale_v, load_sem.at[0])
    load_states = pltpu.make_async_copy(states_hbm, states_v, load_sem.at[1])
    load_text = pltpu.make_async_copy(text_hbm, text_v, load_sem.at[2])
    load_mod = pltpu.make_async_copy(mod_hbm, mod_v, load_sem.at[3])
    load_stale.start()
    load_states.start()
    load_mod.start()
    load_text.start()
    loads = []
    for part in range(D // W_ROWS):
        rows = pl.ds(part * W_ROWS, W_ROWS)
        loads.append(
            pltpu.make_async_copy(weight_hbm.at[rows], weight_v.at[rows], weight_sem.at[part])
        )
        loads[-1].start()

    barrier = pltpu.get_barrier_semaphore()

    @pl.loop(1, BLK)
    def _(step):
        pl.semaphore_signal(
            barrier, inc=1, device_id=(sec, lax.rem(me + step, BLK)), device_id_type=MESH
        )

    @pl.loop(0, BLK)
    def _(step):
        pl.semaphore_signal(
            barrier, inc=1, device_id=(before, lax.rem(me + step, BLK)), device_id_type=MESH
        )

    core = lax.rem(me, 2)
    chip = me // 2
    sibling = me + 1 - 2 * core
    spare_index = lax.rem(chip, 4)
    has_spare = spare_index < SPARE_HEADS
    first_block = SPARE * (2 * (me // 8) + core)

    def spare_device(index, part):
        return 8 * (part // 2) + 2 * index + lax.rem(part, 2)

    def peer(step):
        ring = step // 4
        up = jnp.where(ring == 0, 2, jnp.where(ring == 1, 1, jnp.where(ring == 2, 3, 0)))
        rest = lax.rem(step, 4)
        to_x = lax.rem(me // 8 + 1 - rest // 2, 2)
        to_y = lax.rem(chip + up, 4)
        to_core = lax.rem(core + 1 - lax.rem(rest, 2), 2)
        return 8 * to_x + 2 * to_y + to_core

    def remote(source, target, send, recv, to, section=None):
        return pltpu.make_async_remote_copy(
            src_ref=source,
            dst_ref=target,
            send_sem=send,
            recv_sem=recv,
            device_id=(sec if section is None else section, to),
            device_id_type=MESH,
        )

    def arrived(ref, sem):
        pltpu.make_async_copy(ref, ref, sem).wait()

    def send_main(kind):
        @pl.loop(0, BLK - 1)
        def _(step):
            to = peer(step)
            remote(
                main_send.at[kind, to],
                kv.at[0, kind, me],
                main_ssem.at[kind],
                main_rsem.at[kind],
                to,
            ).start()

        pltpu.make_async_copy(
            main_send.at[kind, me], kv.at[0, kind, me], main_rsem.at[kind]
        ).start()

    def spare_copy(kind, to_chip):
        return remote(
            spare_send.at[kind, lax.rem(to_chip, 4)],
            kv.at[1, kind, 8 * core + chip],
            spare_ssem.at[kind, to_chip],
            spare_rsem.at[kind],
            2 * to_chip + core,
        )

    def send_spare(kind):
        @pl.loop(0, BLK // 2)
        def _(step):
            to_chip = peer(2 * step) // 2

            @pl.when(jnp.logical_and(to_chip != chip, lax.rem(to_chip, 4) < SPARE_HEADS))
            def _():
                spare_copy(kind, to_chip).start()

        @pl.when(has_spare)
        def _():
            pltpu.make_async_copy(
                spare_send.at[kind, spare_index],
                kv.at[1, kind, 8 * core + chip],
                spare_rsem.at[kind],
            ).start()

    def pass_copy(kind):
        block = kv.at[1, kind, pl.ds(8 * core, 8)]
        return remote(block, block, pass_ssem.at[kind], pass_rsem.at[kind], sibling)

    def pass_spare(kind):
        @pl.when(has_spare)
        def _():
            arrived(kv.at[1, kind, pl.ds(8 * core, 8)], spare_rsem.at[kind])
            pass_copy(kind).start()

    load_stale.wait()
    first_worked = patch_ref[0] == 0
    for index in range(HEADS):
        cols = slice(128 * index, 128 * index + 128)
        entries_v[:, cols] = jnp.where(first_worked, stale_v[1, :, cols], stale_v[0, :, cols])
    pack_heads(entries_v, main_send.at[0], spare_send.at[0])
    pl.semaphore_wait(barrier, 2 * BLK - 1)
    send_main(0)

    load_text.wait()
    load_mod.wait()
    row = step_ref[0]
    text_normed = (
        layer_norm(text_v[...].astype(F32).T) * (1.0 + mod_v[row, 4]) + mod_v[row, 3]
    ).astype(BF)
    text_part = lax.dot_general(
        text_weight_ref[...],
        text_normed,
        (((1,), (1,)), ((), ())),
        preferred_element_type=F32,
    )
    for unit in range(TEXT_COLS // 8):
        eight = text_part[8 * unit : 8 * unit + 8]
        text_send[unit] = jnp.concatenate([eight[:, :128], eight[:, 128:]], axis=0).astype(BF)

    second_half = me // 8
    half_units = TEXT_COLS // 8

    def text_pieces(place):
        pieces = []
        unit = half_units * place
        while unit < half_units * (place + 1):
            head = unit // 8
            end = min(8 * head + 8, half_units * (place + 1))
            pieces.append((unit - half_units * place, end - unit, head, unit % 8))
            unit = end
        return pieces

    def text_copies(act, act_local):
        for place in range(8):

            @pl.when(lax.rem(me, 8) == place)
            def _():
                for number, (row, units, head, to_row) in enumerate(text_pieces(place)):
                    spare = head >= BLK
                    source = text_send.at[pl.ds(row, units)]
                    target = text_recv.at[int(spare), pl.ds(8 * second_half + to_row, units)]

                    @pl.loop(0, SPARE_DEVICES if spare else 1)
                    def _(step):
                        to = spare_device(head - BLK, step) if spare else jnp.int32(head)

                        @pl.when(to != me)
                        def _():
                            act(
                                remote(
                                    source,
                                    target,
                                    text_ssem.at[number, step],
                                    text_rsem.at[int(spare)],
                                    to,
                                )
                            )

                        @pl.when(to == me)
                        def _():
                            act_local(source, target, text_rsem.at[int(spare)])

    text_copies(
        lambda copy: copy.start(),
        lambda source, target, sem: pltpu.make_async_copy(source, target, sem).start(),
    )

    slot_there = lax.rem(me, SPARE)

    def spare_target(index):
        return spare_device(index, me // SPARE)

    def query_copy(index):
        return remote(
            q_send.at[BLK + index],
            q_spare.at[slot_there],
            q_ssem2.at[index],
            q_rsem2.at[slot_there],
            spare_target(index),
        )

    def state_rows(head):
        return states_v.at[pl.ds(pl.multiple_of(HD * head, HD), HD)]

    def state_copy(index):
        return remote(
            state_rows(BLK + index),
            state_recv.at[BLK + slot_there],
            state_ssem2.at[index],
            state_rsem2.at[slot_there],
            spare_target(index),
        )

    load_states.wait()
    normed = (
        layer_norm(states_v[...].astype(F32).T) * (1.0 + mod_v[row, 1]) + mod_v[row, 0]
    ).astype(BF)
    for load in loads:
        load.wait()

    block_ones = (
        (lax.broadcasted_iota(jnp.int32, (128, 128), 0) < HD)
        == (lax.broadcasted_iota(jnp.int32, (128, 128), 1) < HD)
    ).astype(BF)
    query_gain = query_gain_ref[...]
    key_gain = key_gain_ref[...]

    def project(first, last):
        proj_v[:, first:last] = jnp.dot(
            normed, weight_v[:, first:last], preferred_element_type=F32
        )

    def normed_tile(index):
        value = proj_v[:, 128 * index : 128 * index + 128]
        square = value * value
        high = square.astype(BF)
        low = (square - high.astype(F32)).astype(BF)
        mean = (
            jnp.dot(high, block_ones, preferred_element_type=F32)
            + jnp.dot(low, block_ones, preferred_element_type=F32)
        ) * (1.0 / HD)
        gain = jnp.concatenate(
            [
                query_gain if index < 10 else key_gain,
                query_gain if index < 9 else key_gain,
            ],
            axis=1,
        )
        return value * lax.rsqrt(mean + 1e-06) * gain

    low64 = low_half(HD)
    project(0, 1280)
    for index in range(10):
        value = normed_tile(index)
        if index == 9:
            proj_v[:, 128 * index : 128 * index + 128] = value
        top, bottom = value[:HD], value[HD:]
        even = jnp.where(low64, top, swap_halves(bottom))
        q_send[2 * index] = (even.astype(BF).astype(F32) * 0.125).astype(BF)
        if index < 9:
            odd = jnp.where(low64, swap_halves(top), bottom)
            q_send[2 * index + 1] = (odd.astype(BF).astype(F32) * 0.125).astype(BF)

    @pl.loop(0, BLK - 1)
    def _(step):
        to = peer(step)
        remote(q_send.at[to], q_recv.at[me], q_ssem, q_rsem, to).start()

    pltpu.make_async_copy(q_send.at[me], q_recv.at[me], q_rsem).start()

    for index in range(SPARE_HEADS):

        @pl.when(spare_target(index) != me)
        def _():
            query_copy(index).start()

        @pl.when(spare_target(index) == me)
        def _():
            pltpu.make_async_copy(
                q_send.at[BLK + index], q_spare.at[slot_there], q_rsem2.at[slot_there]
            ).start()

    @pl.loop(0, BLK - 1)
    def _(step):
        to = peer(step)
        remote(state_rows(to), state_recv.at[me], state_ssem, state_rsem, to).start()

    pltpu.make_async_copy(state_rows(me), state_recv.at[me], state_rsem).start()
    for index in range(SPARE_HEADS):

        @pl.when(spare_target(index) != me)
        def _():
            state_copy(index).start()

        @pl.when(spare_target(index) == me)
        def _():
            pltpu.make_async_copy(
                state_rows(BLK + index), state_recv.at[BLK + slot_there], state_rsem2.at[slot_there]
            ).start()

    project(1280, 2432)
    project(2432, 3648)
    low = low_half(TOK)

    def swapped_tile(index):
        if index == 9 or index >= 19:
            return swap_halves(proj_v[:, 128 * index : 128 * index + 128])
        return swap_halves(normed_tile(index))

    left = swapped_tile(9)
    for index in range(HEADS):
        right = swapped_tile(10 + index)
        fresh_v[:, 128 * index : 128 * index + 128] = jnp.where(low, left, right).astype(BF)
        left = right
    fresh_copy = pltpu.make_async_copy(fresh_v, fresh_hbm, fresh_sem)
    fresh_copy.start()
    pack_heads(fresh_v, main_send.at[1], spare_send.at[1])
    send_main(1)

    send_spare(0)
    send_spare(1)

    one = jnp.ones((1, 128), F32)
    low1 = low_half(1)
    gate_pad = jnp.concatenate([mod_v[row, 2], jnp.zeros((1, 64), F32)], axis=1)
    for head in range(HEADS):
        gate = gate_pad[:, 128 * (head // 2) : 128 * (head // 2) + 128]
        if head % 2 == 0:
            gate = swap_halves(jnp.broadcast_to(gate, (8, 128)))[0:1]
        gate_v[head : head + 1, :] = jnp.where(low1, one, gate)

    arrived(q_recv, q_rsem)

    def spread_queries(packed, row):
        value = packed.astype(F32)
        zero = jnp.zeros_like(value)
        q_all[pl.ds(row, HD)] = jnp.where(low64, value, zero).astype(BF)
        q_all[pl.ds(row + HD, HD)] = jnp.where(low64, swap_halves(value), zero).astype(BF)

    @pl.loop(0, BLK)
    def _(step):
        spread_queries(q_recv[step], pl.multiple_of(step * TOK, TOK))

    @pl.when(has_spare)
    def _():
        for slot in range(SPARE):
            arrived(q_spare.at[slot], q_rsem2.at[slot])
            spread_queries(q_spare[slot], ROWS + slot * TOK)

    def with_ones(entries):
        return jnp.where(
            low_half(entries.shape[0]), jnp.ones(entries.shape, F32), entries.astype(F32)
        ).astype(BF)

    def attend(rows, entries, values):
        scores = lax.dot_general(
            q_all[rows], entries, (((1,), (1,)), ((), ())), preferred_element_type=F32
        )
        powers = jnp.exp(scores).astype(BF)
        return jnp.dot(powers, values, preferred_element_type=F32)

    low256 = low_half(TEXT)
    text_gain = jnp.concatenate([text_gain_ref[...], jnp.ones((1, HD), F32)], axis=1)

    def take_text(which):
        arrived(text_recv.at[which], text_rsem.at[which])
        tiles = text_recv[which].astype(F32)
        halves = [tiles[:, 8 * half : 8 * half + 8].reshape(128, 128) for half in range(2)]
        value = jnp.concatenate([halves[0].T, halves[1].T], axis=0)
        square = jnp.where(low256, value * value, 0.0)
        mean = jnp.sum(square, axis=1, keepdims=True) * (1.0 / HD)
        scaled = value * lax.rsqrt(mean + 1e-06) * text_gain
        entries = jnp.where(low256, scaled, value).astype(BF)
        kv[which, 0, BLK] = entries[:TOK]
        kv[which, 1, BLK] = entries[TOK:]

    take_text(0)

    @pl.when(has_spare)
    def _():
        take_text(1)

    acc[...] = jnp.zeros_like(acc)
    arrived(kv.at[0, 0, pl.ds(0, BLK)], main_rsem.at[0])

    tiles = ROWS // QT
    per_tile = QT // TOK

    def result_copy(slot):
        main = slot < BLK
        head = jnp.where(main, me, BLK + spare_index)
        target = out_hbm.at[pl.ds(pl.multiple_of(HD * head, HD), HD)]
        block = jnp.where(main, slot, first_block + slot - BLK)
        return remote(out_send.at[slot], target, out_ssem.at[slot], out_rsem, block, after)

    @pl.loop(0, 2 * tiles + 2)
    def _(item):
        @pl.when(item == tiles)
        def _():
            arrived(kv.at[0, 1, pl.ds(0, BLK)], main_rsem.at[1])
            arrived(state_recv.at[pl.ds(0, BLK)], state_rsem)

        @pl.when(item == tiles + 2)
        def _():
            pass_spare(0)

        @pl.when(item == 2 * tiles)
        def _():
            pass_spare(1)

        main = item < 2 * tiles
        kind = jnp.where(main, item // tiles, item - 2 * tiles)
        which = jnp.where(main, 0, 1)
        step = jnp.where(main, lax.rem(me + item, tiles), tiles)

        @pl.when(jnp.logical_and(has_spare, jnp.logical_not(main)))
        def _():
            arrived(kv.at[1, kind, pl.ds(8 * (1 - core), 8)], pass_rsem.at[kind])

        @pl.when(jnp.logical_or(has_spare, main))
        def _():
            rows = pl.ds(pl.multiple_of(step * QT, QT), QT)
            entries = kv[which, kind].reshape((BLK + 1) * TOK, 128)
            acc[rows] += attend(rows, entries, with_ones(entries))

        @pl.when(jnp.logical_and(has_spare, item == 2 * tiles + 1))
        def _():
            for slot in range(SPARE):
                arrived(state_recv.at[BLK + slot], state_rsem2.at[slot])

        @pl.when(jnp.logical_and(kind == 1, jnp.logical_or(has_spare, main)))
        def _():
            gate = gate_v[pl.ds(jnp.where(main, me, BLK + spare_index), 1), :]

            @pl.loop(0, per_tile)
            def _(part):
                slot = step * per_tile + part
                value = acc[pl.ds(pl.multiple_of(slot * TOK, TOK), TOK)] * gate
                turned = value.T
                out_send[slot] = (
                    state_recv[slot].astype(F32) + turned[HD:] / turned[:HD]
                ).astype(BF)
                result_copy(slot).start()

    arrived(out_hbm, out_rsem)

    fresh_copy.wait()
    for kind in range(2):
        arrived(main_send.at[kind, pl.ds(0, BLK - 1)], main_ssem.at[kind])

        @pl.loop(0, BLK // 2)
        def _(to_chip):
            @pl.when(jnp.logical_and(to_chip != chip, lax.rem(to_chip, 4) < SPARE_HEADS))
            def _():
                spare_copy(kind, to_chip).wait_send()

    arrived(q_send.at[pl.ds(0, BLK - 1)], q_ssem)
    arrived(state_recv.at[pl.ds(0, BLK - 1)], state_ssem)
    for index in range(SPARE_HEADS):

        @pl.when(spare_target(index) != me)
        def _():
            query_copy(index).wait_send()
            state_copy(index).wait_send()

    text_copies(lambda copy: copy.wait_send(), lambda *_: None)

    @pl.loop(0, BLK)
    def _(slot):
        result_copy(slot).wait_send()

    @pl.when(has_spare)
    def _():
        for slot in range(SPARE):
            result_copy(BLK + slot).wait_send()
        for kind in range(2):
            pass_copy(kind).wait_send()


def write_results(raw_states, raw_fresh, states_out, fresh_out, states_v, fresh_v, sems):
    loads = (
        pltpu.make_async_copy(raw_fresh, fresh_v, sems.at[0]),
        pltpu.make_async_copy(raw_states, states_v, sems.at[1]),
    )
    stores = (
        pltpu.make_async_copy(fresh_v, fresh_out, sems.at[0]),
        pltpu.make_async_copy(states_v, states_out, sems.at[1]),
    )
    for load in loads:
        load.start()
    for load, store in zip(loads, stores):
        load.wait()
        store.start()
    for store in stores:
        store.wait()


def body(
    sections,
    states,
    image_weight,
    text_weight,
    text_states,
    stale_cache,
    modulation,
    query_gain,
    key_gain,
    text_gain,
    timestep,
    layer_patch_index,
):
    vmem = pl.BlockSpec(memory_space=pltpu.VMEM)
    anywhere = pl.BlockSpec(memory_space=pl.ANY)
    dma = pltpu.SemaphoreType.DMA
    next_states, fresh = pl.pallas_call(
        functools.partial(kernel, sections),
        out_shape=(
            jax.ShapeDtypeStruct((D, TOK), BF),
            jax.ShapeDtypeStruct((TOK, 2 * D), BF),
        ),
        in_specs=[
            pl.BlockSpec(memory_space=pltpu.SMEM),
            pl.BlockSpec(memory_space=pltpu.SMEM),
            anywhere,
            anywhere,
            vmem,
            anywhere,
            anywhere,
            anywhere,
            vmem,
            vmem,
            vmem,
        ],
        out_specs=(anywhere, anywhere),
        scratch_shapes=[
            pltpu.VMEM((D, TOK), BF),
            pltpu.VMEM((D, 3 * D), BF),
            pltpu.VMEM((D, TEXT), BF),
            pltpu.VMEM((2, TOK, 2 * D), BF),
            pltpu.VMEM((modulation.shape[0], 5, 1, D), F32),
            pltpu.VMEM((TOK, 2 * D), BF),
            pltpu.VMEM((TOK, 3 * D + 64), F32),
            pltpu.VMEM((TOK, 2 * D), BF),
            pltpu.VMEM((2, BLK, TOK, 128), BF),
            pltpu.VMEM((2, 2, BLK + 1, TOK, 128), BF),
            pltpu.VMEM((2, SPARE_HEADS, TOK, 128), BF),
            pltpu.VMEM((HEADS, HD, 128), BF),
            pltpu.VMEM((BLK, HD, 128), BF),
            pltpu.VMEM((SPARE, HD, 128), BF),
            pltpu.VMEM((ROWS + SPARE_ROWS, 128), BF),
            pltpu.VMEM((BLK + SPARE, HD, 128), BF),
            pltpu.VMEM((ROWS + SPARE_ROWS, 128), F32),
            pltpu.VMEM((TEXT_COLS // 8, 16, 128), BF),
            pltpu.VMEM((2, 16, 16, 128), BF),
            pltpu.VMEM((24, 128), F32),
            pltpu.VMEM((BLK + SPARE, HD, 128), BF),
            dma((4,)),
            dma((D // W_ROWS,)),
            dma((2,)),
            dma((2,)),
            dma((2, BLK // 2)),
            dma((2,)),
            dma((2,)),
            dma((2,)),
            dma,
            dma,
            dma((SPARE_HEADS,)),
            dma((SPARE,)),
            dma,
            dma,
            dma((SPARE_HEADS,)),
            dma((SPARE,)),
            dma((4, SPARE_DEVICES)),
            dma((2,)),
            dma((BLK + SPARE,)),
            dma,
            dma,
        ],
        compiler_params=pltpu.CompilerParams(
            collective_id=0, has_side_effects=True, vmem_limit_bytes=56 * 1024 * 1024
        ),
    )(
        layer_patch_index,
        timestep,
        jnp.swapaxes(states[0], 0, 1),
        image_weight[0],
        jnp.swapaxes(text_weight[0], 0, 1),
        jnp.swapaxes(text_states[0], 0, 1),
        stale_cache[0],
        jnp.swapaxes(modulation, 1, 2),
        query_gain,
        key_gain,
        text_gain,
    )
    next_states, fresh = pl.pallas_call(
        write_results,
        out_shape=(
            jax.ShapeDtypeStruct((D, TOK), BF),
            jax.ShapeDtypeStruct((TOK, 2 * D), BF),
        ),
        in_specs=[anywhere, anywhere],
        out_specs=(anywhere, anywhere),
        scratch_shapes=[pltpu.VMEM((D, TOK), BF), pltpu.VMEM((TOK, 2 * D), BF), dma((2,))],
        compiler_params=pltpu.CompilerParams(vmem_limit_bytes=60 * 1024 * 1024),
    )(next_states, fresh)
    return (jnp.swapaxes(next_states, 0, 1)[None], fresh[None])


def solution(mesh):
    in_specs = (
        P("section", "blk", None),
        P("section", None, None),
        P("section", None, "blk"),
        P("section", None, None),
        P("section", None, "blk", None),
        P(None, "section", None, None),
        P("section", None),
        P("section", None),
        P("section", None),
        P("section"),
        P("section"),
    )
    out_specs = (P("section", "blk", None), P("section", "blk", None))
    return jax.shard_map(
        functools.partial(body, mesh.shape["section"]),
        mesh=mesh,
        in_specs=in_specs,
        out_specs=out_specs,
        check_vma=False,
    )
```

```python
import functools

import jax
import jax.numpy as jnp
from jax import lax
from jax.experimental import pallas as pl
from jax.experimental.pallas import tpu as pltpu
from jax.sharding import PartitionSpec as P

MESH = pl.DeviceIdType.MESH
BF = jnp.bfloat16
F32 = jnp.float32

D = 1216
HEADS = 19
HD = 64
TOK = 128
TEXT = 256
BLK = 16
TEXT_COLS = 152
SPARE = 4
ROWS = BLK * TOK
SPARE_ROWS = SPARE * TOK
W_ROWS = 304
SPARE_DEVICES = 4
SPARE_HEADS = 3
QT = 512


def low_half(rows):
    return lax.broadcasted_iota(jnp.int32, (rows, 128), 1) < HD


def swap_halves(value):
    return pltpu.roll(value, HD, axis=1)


def layer_norm(values):
    center = values - jnp.mean(values, axis=-1, keepdims=True)
    return center * lax.rsqrt(jnp.mean(center * center, axis=-1, keepdims=True) + 1e-06)


def pack_heads(source, mains, spares):
    low = low_half(TOK)

    def tile(index):
        return source[:, 128 * index : 128 * index + 128].astype(F32)

    for head in range(HEADS):
        half = head // 2
        if head % 2 == 0:
            packed = jnp.where(low, tile(half), tile(9 + half))
        else:
            packed = swap_halves(jnp.where(low, tile(10 + half), tile(half)))
        if head < BLK:
            mains[head] = packed.astype(BF)
        else:
            spares[head - BLK] = packed.astype(BF)


def kernel(
    sections,
    patch_ref,
    step_ref,
    states_hbm,
    weight_hbm,
    text_weight_ref,
    text_hbm,
    stale_hbm,
    mod_hbm,
    query_gain_ref,
    key_gain_ref,
    text_gain_ref,
    out_hbm,
    fresh_hbm,
    states_v,
    weight_v,
    text_v,
    stale_v,
    mod_v,
    entries_v,
    proj_v,
    fresh_v,
    main_send,
    kv,
    spare_send,
    q_send,
    q_recv,
    q_spare,
    q_all,
    state_recv,
    acc,
    text_send,
    text_recv,
    gate_v,
    out_send,
    load_sem,
    weight_sem,
    main_ssem,
    main_rsem,
    spare_ssem,
    spare_rsem,
    pass_ssem,
    pass_rsem,
    q_ssem,
    q_rsem,
    q_ssem2,
    q_rsem2,
    state_ssem,
    state_rsem,
    state_ssem2,
    state_rsem2,
    text_ssem,
    text_rsem,
    out_ssem,
    out_rsem,
    fresh_sem,
):
    sec = lax.axis_index("section")
    me = lax.axis_index("blk")
    after = lax.rem(sec + 1, sections)
    before = lax.rem(sec + sections - 1, sections)

    load_stale = pltpu.make_async_copy(stale_hbm, stale_v, load_sem.at[0])
    load_states = pltpu.make_async_copy(states_hbm, states_v, load_sem.at[1])
    load_text = pltpu.make_async_copy(text_hbm, text_v, load_sem.at[2])
    load_mod = pltpu.make_async_copy(mod_hbm, mod_v, load_sem.at[3])
    load_stale.start()
    load_states.start()
    load_mod.start()
    load_text.start()
    loads = []
    for part in range(D // W_ROWS):
        rows = pl.ds(part * W_ROWS, W_ROWS)
        loads.append(
            pltpu.make_async_copy(weight_hbm.at[rows], weight_v.at[rows], weight_sem.at[part])
        )
        loads[-1].start()

    barrier = pltpu.get_barrier_semaphore()

    @pl.loop(1, BLK)
    def _(step):
        pl.semaphore_signal(
            barrier, inc=1, device_id=(sec, lax.rem(me + step, BLK)), device_id_type=MESH
        )

    @pl.loop(0, BLK)
    def _(step):
        pl.semaphore_signal(
            barrier, inc=1, device_id=(before, lax.rem(me + step, BLK)), device_id_type=MESH
        )

    core = lax.rem(me, 2)
    chip = me // 2
    sibling = me + 1 - 2 * core
    spare_index = lax.rem(chip, 4)
    has_spare = spare_index < SPARE_HEADS
    first_block = SPARE * (2 * (me // 8) + core)

    def spare_device(index, part):
        return 8 * (part // 2) + 2 * index + lax.rem(part, 2)

    def peer(step):
        ring = step // 4
        up = jnp.where(ring == 0, 2, jnp.where(ring == 1, 1, jnp.where(ring == 2, 3, 0)))
        rest = lax.rem(step, 4)
        to_x = lax.rem(me // 8 + 1 - rest // 2, 2)
        to_y = lax.rem(chip + up, 4)
        to_core = lax.rem(core + 1 - lax.rem(rest, 2), 2)
        return 8 * to_x + 2 * to_y + to_core

    def remote(source, target, send, recv, to, section=None):
        return pltpu.make_async_remote_copy(
            src_ref=source,
            dst_ref=target,
            send_sem=send,
            recv_sem=recv,
            device_id=(sec if section is None else section, to),
            device_id_type=MESH,
        )

    def arrived(ref, sem):
        pltpu.make_async_copy(ref, ref, sem).wait()

    def send_main(kind):
        @pl.loop(0, BLK - 1)
        def _(step):
            to = peer(step)
            remote(
                main_send.at[kind, to],
                kv.at[0, kind, me],
                main_ssem.at[kind],
                main_rsem.at[kind],
                to,
            ).start()

        pltpu.make_async_copy(
            main_send.at[kind, me], kv.at[0, kind, me], main_rsem.at[kind]
        ).start()

    def spare_copy(kind, to_chip):
        return remote(
            spare_send.at[kind, lax.rem(to_chip, 4)],
            kv.at[1, kind, 8 * core + chip],
            spare_ssem.at[kind, to_chip],
            spare_rsem.at[kind],
            2 * to_chip + core,
        )

    def send_spare(kind):
        @pl.loop(0, BLK // 2)
        def _(step):
            to_chip = peer(2 * step) // 2

            @pl.when(jnp.logical_and(to_chip != chip, lax.rem(to_chip, 4) < SPARE_HEADS))
            def _():
                spare_copy(kind, to_chip).start()

        @pl.when(has_spare)
        def _():
            pltpu.make_async_copy(
                spare_send.at[kind, spare_index],
                kv.at[1, kind, 8 * core + chip],
                spare_rsem.at[kind],
            ).start()

    def pass_copy(kind):
        block = kv.at[1, kind, pl.ds(8 * core, 8)]
        return remote(block, block, pass_ssem.at[kind], pass_rsem.at[kind], sibling)

    def pass_spare(kind):
        @pl.when(has_spare)
        def _():
            arrived(kv.at[1, kind, pl.ds(8 * core, 8)], spare_rsem.at[kind])
            pass_copy(kind).start()

    load_stale.wait()
    first_worked = patch_ref[0] == 0
    for index in range(HEADS):
        cols = slice(128 * index, 128 * index + 128)
        entries_v[:, cols] = jnp.where(first_worked, stale_v[1, :, cols], stale_v[0, :, cols])
    pack_heads(entries_v, main_send.at[0], spare_send.at[0])
    pl.semaphore_wait(barrier, 2 * BLK - 1)
    send_main(0)

    load_text.wait()
    load_mod.wait()
    row = step_ref[0]
    text_normed = (
        layer_norm(text_v[...].astype(F32).T) * (1.0 + mod_v[row, 4]) + mod_v[row, 3]
    ).astype(BF)
    text_part = lax.dot_general(
        text_weight_ref[...],
        text_normed,
        (((1,), (1,)), ((), ())),
        preferred_element_type=F32,
    )
    for unit in range(TEXT_COLS // 8):
        eight = text_part[8 * unit : 8 * unit + 8]
        text_send[unit] = jnp.concatenate([eight[:, :128], eight[:, 128:]], axis=0).astype(BF)

    second_half = me // 8
    half_units = TEXT_COLS // 8

    def text_pieces(place):
        pieces = []
        unit = half_units * place
        while unit < half_units * (place + 1):
            head = unit // 8
            end = min(8 * head + 8, half_units * (place + 1))
            pieces.append((unit - half_units * place, end - unit, head, unit % 8))
            unit = end
        return pieces

    def text_copies(act, act_local):
        for place in range(8):

            @pl.when(lax.rem(me, 8) == place)
            def _():
                for number, (row, units, head, to_row) in enumerate(text_pieces(place)):
                    spare = head >= BLK
                    source = text_send.at[pl.ds(row, units)]
                    target = text_recv.at[int(spare), pl.ds(8 * second_half + to_row, units)]

                    @pl.loop(0, SPARE_DEVICES if spare else 1)
                    def _(step):
                        to = spare_device(head - BLK, step) if spare else jnp.int32(head)

                        @pl.when(to != me)
                        def _():
                            act(
                                remote(
                                    source,
                                    target,
                                    text_ssem.at[number, step],
                                    text_rsem.at[int(spare)],
                                    to,
                                )
                            )

                        @pl.when(to == me)
                        def _():
                            act_local(source, target, text_rsem.at[int(spare)])

    text_copies(
        lambda copy: copy.start(),
        lambda source, target, sem: pltpu.make_async_copy(source, target, sem).start(),
    )

    slot_there = lax.rem(me, SPARE)

    def spare_target(index):
        return spare_device(index, me // SPARE)

    def query_copy(index):
        return remote(
            q_send.at[BLK + index],
            q_spare.at[slot_there],
            q_ssem2.at[index],
            q_rsem2.at[slot_there],
            spare_target(index),
        )

    def state_rows(head):
        return states_v.at[pl.ds(pl.multiple_of(HD * head, HD), HD)]

    def state_copy(index):
        return remote(
            state_rows(BLK + index),
            state_recv.at[BLK + slot_there],
            state_ssem2.at[index],
            state_rsem2.at[slot_there],
            spare_target(index),
        )

    load_states.wait()
    normed = (
        layer_norm(states_v[...].astype(F32).T) * (1.0 + mod_v[row, 1]) + mod_v[row, 0]
    ).astype(BF)
    for load in loads:
        load.wait()

    block_ones = (
        (lax.broadcasted_iota(jnp.int32, (128, 128), 0) < HD)
        == (lax.broadcasted_iota(jnp.int32, (128, 128), 1) < HD)
    ).astype(BF)
    query_gain = query_gain_ref[...]
    key_gain = key_gain_ref[...]

    def project(first, last):
        proj_v[:, first:last] = jnp.dot(
            normed, weight_v[:, first:last], preferred_element_type=F32
        )

    def normed_tile(index):
        value = proj_v[:, 128 * index : 128 * index + 128]
        square = value * value
        high = square.astype(BF)
        low = (square - high.astype(F32)).astype(BF)
        mean = (
            jnp.dot(high, block_ones, preferred_element_type=F32)
            + jnp.dot(low, block_ones, preferred_element_type=F32)
        ) * (1.0 / HD)
        gain = jnp.concatenate(
            [
                query_gain if index < 10 else key_gain,
                query_gain if index < 9 else key_gain,
            ],
            axis=1,
        )
        return value * lax.rsqrt(mean + 1e-06) * gain

    low64 = low_half(HD)
    project(0, 1280)
    for index in range(10):
        value = normed_tile(index)
        if index == 9:
            proj_v[:, 128 * index : 128 * index + 128] = value
        top, bottom = value[:HD], value[HD:]
        even = jnp.where(low64, top, swap_halves(bottom))
        q_send[2 * index] = (even.astype(BF).astype(F32) * 0.125).astype(BF)
        if index < 9:
            odd = jnp.where(low64, swap_halves(top), bottom)
            q_send[2 * index + 1] = (odd.astype(BF).astype(F32) * 0.125).astype(BF)

    @pl.loop(0, BLK - 1)
    def _(step):
        to = peer(step)
        remote(q_send.at[to], q_recv.at[me], q_ssem, q_rsem, to).start()

    pltpu.make_async_copy(q_send.at[me], q_recv.at[me], q_rsem).start()

    for index in range(SPARE_HEADS):

        @pl.when(spare_target(index) != me)
        def _():
            query_copy(index).start()

        @pl.when(spare_target(index) == me)
        def _():
            pltpu.make_async_copy(
                q_send.at[BLK + index], q_spare.at[slot_there], q_rsem2.at[slot_there]
            ).start()

    @pl.loop(0, BLK - 1)
    def _(step):
        to = peer(step)
        remote(state_rows(to), state_recv.at[me], state_ssem, state_rsem, to).start()

    pltpu.make_async_copy(state_rows(me), state_recv.at[me], state_rsem).start()
    for index in range(SPARE_HEADS):

        @pl.when(spare_target(index) != me)
        def _():
            state_copy(index).start()

        @pl.when(spare_target(index) == me)
        def _():
            pltpu.make_async_copy(
                state_rows(BLK + index), state_recv.at[BLK + slot_there], state_rsem2.at[slot_there]
            ).start()

    project(1280, 2432)
    project(2432, 3648)
    low = low_half(TOK)

    def swapped_tile(index):
        if index == 9 or index >= 19:
            return swap_halves(proj_v[:, 128 * index : 128 * index + 128])
        return swap_halves(normed_tile(index))

    left = swapped_tile(9)
    for index in range(HEADS):
        right = swapped_tile(10 + index)
        fresh_v[:, 128 * index : 128 * index + 128] = jnp.where(low, left, right).astype(BF)
        left = right
    fresh_copy = pltpu.make_async_copy(fresh_v, fresh_hbm, fresh_sem)
    fresh_copy.start()
    pack_heads(fresh_v, main_send.at[1], spare_send.at[1])
    send_main(1)

    send_spare(0)
    send_spare(1)

    one = jnp.ones((1, 128), F32)
    low1 = low_half(1)
    gate_pad = jnp.concatenate([mod_v[row, 2], jnp.zeros((1, 64), F32)], axis=1)
    for head in range(HEADS):
        gate = gate_pad[:, 128 * (head // 2) : 128 * (head // 2) + 128]
        if head % 2 == 0:
            gate = swap_halves(jnp.broadcast_to(gate, (8, 128)))[0:1]
        gate_v[head : head + 1, :] = jnp.where(low1, one, gate)

    arrived(q_recv, q_rsem)

    def spread_queries(packed, row):
        value = packed.astype(F32)
        zero = jnp.zeros_like(value)
        q_all[pl.ds(row, HD)] = jnp.where(low64, value, zero).astype(BF)
        q_all[pl.ds(row + HD, HD)] = jnp.where(low64, swap_halves(value), zero).astype(BF)

    @pl.loop(0, BLK)
    def _(step):
        spread_queries(q_recv[step], pl.multiple_of(step * TOK, TOK))

    @pl.when(has_spare)
    def _():
        for slot in range(SPARE):
            arrived(q_spare.at[slot], q_rsem2.at[slot])
            spread_queries(q_spare[slot], ROWS + slot * TOK)

    def with_ones(entries):
        return jnp.where(
            low_half(entries.shape[0]), jnp.ones(entries.shape, F32), entries.astype(F32)
        ).astype(BF)

    def attend(rows, entries, values):
        scores = lax.dot_general(
            q_all[rows], entries, (((1,), (1,)), ((), ())), preferred_element_type=F32
        )
        powers = jnp.exp(scores).astype(BF)
        return jnp.dot(powers, values, preferred_element_type=F32)

    low256 = low_half(TEXT)
    text_gain = jnp.concatenate([text_gain_ref[...], jnp.ones((1, HD), F32)], axis=1)

    def take_text(which):
        arrived(text_recv.at[which], text_rsem.at[which])
        tiles = text_recv[which].astype(F32)
        halves = [tiles[:, 8 * half : 8 * half + 8].reshape(128, 128) for half in range(2)]
        value = jnp.concatenate([halves[0].T, halves[1].T], axis=0)
        square = jnp.where(low256, value * value, 0.0)
        mean = jnp.sum(square, axis=1, keepdims=True) * (1.0 / HD)
        scaled = value * lax.rsqrt(mean + 1e-06) * text_gain
        entries = jnp.where(low256, scaled, value).astype(BF)
        kv[which, 0, BLK] = entries[:TOK]
        kv[which, 1, BLK] = entries[TOK:]

    take_text(0)

    @pl.when(has_spare)
    def _():
        take_text(1)

    acc[...] = jnp.zeros_like(acc)
    arrived(kv.at[0, 0, pl.ds(0, BLK)], main_rsem.at[0])

    tiles = ROWS // QT
    per_tile = QT // TOK

    def result_copy(slot):
        main = slot < BLK
        head = jnp.where(main, me, BLK + spare_index)
        target = out_hbm.at[pl.ds(pl.multiple_of(HD * head, HD), HD)]
        block = jnp.where(main, slot, first_block + slot - BLK)
        return remote(out_send.at[slot], target, out_ssem.at[slot], out_rsem, block, after)

    @pl.loop(0, 2 * tiles + 2)
    def _(item):
        @pl.when(item == tiles)
        def _():
            arrived(kv.at[0, 1, pl.ds(0, BLK)], main_rsem.at[1])
            arrived(state_recv.at[pl.ds(0, BLK)], state_rsem)

        @pl.when(item == tiles + 1)
        def _():
            pass_spare(0)

        @pl.when(item == 2 * tiles - 1)
        def _():
            pass_spare(1)

        main = item < 2 * tiles
        kind = jnp.where(main, item // tiles, item - 2 * tiles)
        which = jnp.where(main, 0, 1)
        step = jnp.where(main, lax.rem(me + item, tiles), tiles)

        @pl.when(jnp.logical_and(has_spare, jnp.logical_not(main)))
        def _():
            arrived(kv.at[1, kind, pl.ds(8 * (1 - core), 8)], pass_rsem.at[kind])

        @pl.when(jnp.logical_or(has_spare, main))
        def _():
            rows = pl.ds(pl.multiple_of(step * QT, QT), QT)
            entries = kv[which, kind].reshape((BLK + 1) * TOK, 128)
            acc[rows] += attend(rows, entries, with_ones(entries))

        @pl.when(jnp.logical_and(has_spare, item == 2 * tiles + 1))
        def _():
            for slot in range(SPARE):
                arrived(state_recv.at[BLK + slot], state_rsem2.at[slot])

        @pl.when(jnp.logical_and(kind == 1, jnp.logical_or(has_spare, main)))
        def _():
            gate = gate_v[pl.ds(jnp.where(main, me, BLK + spare_index), 1), :]

            @pl.loop(0, per_tile)
            def _(part):
                slot = step * per_tile + part
                value = acc[pl.ds(pl.multiple_of(slot * TOK, TOK), TOK)] * gate
                turned = value.T
                out_send[slot] = (
                    state_recv[slot].astype(F32) + turned[HD:] / turned[:HD]
                ).astype(BF)
                result_copy(slot).start()

    arrived(out_hbm, out_rsem)

    fresh_copy.wait()
    for kind in range(2):
        arrived(main_send.at[kind, pl.ds(0, BLK - 1)], main_ssem.at[kind])

        @pl.loop(0, BLK // 2)
        def _(to_chip):
            @pl.when(jnp.logical_and(to_chip != chip, lax.rem(to_chip, 4) < SPARE_HEADS))
            def _():
                spare_copy(kind, to_chip).wait_send()

    arrived(q_send.at[pl.ds(0, BLK - 1)], q_ssem)
    arrived(state_recv.at[pl.ds(0, BLK - 1)], state_ssem)
    for index in range(SPARE_HEADS):

        @pl.when(spare_target(index) != me)
        def _():
            query_copy(index).wait_send()
            state_copy(index).wait_send()

    text_copies(lambda copy: copy.wait_send(), lambda *_: None)

    @pl.loop(0, BLK)
    def _(slot):
        result_copy(slot).wait_send()

    @pl.when(has_spare)
    def _():
        for slot in range(SPARE):
            result_copy(BLK + slot).wait_send()
        for kind in range(2):
            pass_copy(kind).wait_send()


def write_results(raw_states, raw_fresh, states_out, fresh_out, states_v, fresh_v, sems):
    loads = (
        pltpu.make_async_copy(raw_fresh, fresh_v, sems.at[0]),
        pltpu.make_async_copy(raw_states, states_v, sems.at[1]),
    )
    stores = (
        pltpu.make_async_copy(fresh_v, fresh_out, sems.at[0]),
        pltpu.make_async_copy(states_v, states_out, sems.at[1]),
    )
    for load in loads:
        load.start()
    for load, store in zip(loads, stores):
        load.wait()
        store.start()
    for store in stores:
        store.wait()


def body(
    sections,
    states,
    image_weight,
    text_weight,
    text_states,
    stale_cache,
    modulation,
    query_gain,
    key_gain,
    text_gain,
    timestep,
    layer_patch_index,
):
    vmem = pl.BlockSpec(memory_space=pltpu.VMEM)
    anywhere = pl.BlockSpec(memory_space=pl.ANY)
    dma = pltpu.SemaphoreType.DMA
    next_states, fresh = pl.pallas_call(
        functools.partial(kernel, sections),
        out_shape=(
            jax.ShapeDtypeStruct((D, TOK), BF),
            jax.ShapeDtypeStruct((TOK, 2 * D), BF),
        ),
        in_specs=[
            pl.BlockSpec(memory_space=pltpu.SMEM),
            pl.BlockSpec(memory_space=pltpu.SMEM),
            anywhere,
            anywhere,
            vmem,
            anywhere,
            anywhere,
            anywhere,
            vmem,
            vmem,
            vmem,
        ],
        out_specs=(anywhere, anywhere),
        scratch_shapes=[
            pltpu.VMEM((D, TOK), BF),
            pltpu.VMEM((D, 3 * D), BF),
            pltpu.VMEM((D, TEXT), BF),
            pltpu.VMEM((2, TOK, 2 * D), BF),
            pltpu.VMEM((modulation.shape[0], 5, 1, D), F32),
            pltpu.VMEM((TOK, 2 * D), BF),
            pltpu.VMEM((TOK, 3 * D + 64), F32),
            pltpu.VMEM((TOK, 2 * D), BF),
            pltpu.VMEM((2, BLK, TOK, 128), BF),
            pltpu.VMEM((2, 2, BLK + 1, TOK, 128), BF),
            pltpu.VMEM((2, SPARE_HEADS, TOK, 128), BF),
            pltpu.VMEM((HEADS, HD, 128), BF),
            pltpu.VMEM((BLK, HD, 128), BF),
            pltpu.VMEM((SPARE, HD, 128), BF),
            pltpu.VMEM((ROWS + SPARE_ROWS, 128), BF),
            pltpu.VMEM((BLK + SPARE, HD, 128), BF),
            pltpu.VMEM((ROWS + SPARE_ROWS, 128), F32),
            pltpu.VMEM((TEXT_COLS // 8, 16, 128), BF),
            pltpu.VMEM((2, 16, 16, 128), BF),
            pltpu.VMEM((24, 128), F32),
            pltpu.VMEM((BLK + SPARE, HD, 128), BF),
            dma((4,)),
            dma((D // W_ROWS,)),
            dma((2,)),
            dma((2,)),
            dma((2, BLK // 2)),
            dma((2,)),
            dma((2,)),
            dma((2,)),
            dma,
            dma,
            dma((SPARE_HEADS,)),
            dma((SPARE,)),
            dma,
            dma,
            dma((SPARE_HEADS,)),
            dma((SPARE,)),
            dma((4, SPARE_DEVICES)),
            dma((2,)),
            dma((BLK + SPARE,)),
            dma,
            dma,
        ],
        compiler_params=pltpu.CompilerParams(
            collective_id=0, has_side_effects=True, vmem_limit_bytes=56 * 1024 * 1024
        ),
    )(
        layer_patch_index,
        timestep,
        jnp.swapaxes(states[0], 0, 1),
        image_weight[0],
        jnp.swapaxes(text_weight[0], 0, 1),
        jnp.swapaxes(text_states[0], 0, 1),
        stale_cache[0],
        jnp.swapaxes(modulation, 1, 2),
        query_gain,
        key_gain,
        text_gain,
    )
    next_states, fresh = pl.pallas_call(
        write_results,
        out_shape=(
            jax.ShapeDtypeStruct((D, TOK), BF),
            jax.ShapeDtypeStruct((TOK, 2 * D), BF),
        ),
        in_specs=[anywhere, anywhere],
        out_specs=(anywhere, anywhere),
        scratch_shapes=[pltpu.VMEM((D, TOK), BF), pltpu.VMEM((TOK, 2 * D), BF), dma((2,))],
        compiler_params=pltpu.CompilerParams(vmem_limit_bytes=60 * 1024 * 1024),
    )(next_states, fresh)
    return (jnp.swapaxes(next_states, 0, 1)[None], fresh[None])


def solution(mesh):
    in_specs = (
        P("section", "blk", None),
        P("section", None, None),
        P("section", None, "blk"),
        P("section", None, None),
        P("section", None, "blk", None),
        P(None, "section", None, None),
        P("section", None),
        P("section", None),
        P("section", None),
        P("section"),
        P("section"),
    )
    out_specs = (P("section", "blk", None), P("section", "blk", None))
    return jax.shard_map(
        functools.partial(body, mesh.shape["section"]),
        mesh=mesh,
        in_specs=in_specs,
        out_specs=out_specs,
        check_vma=False,
    )
```

```python
import functools

import jax
import jax.numpy as jnp
from jax import lax
from jax.experimental import pallas as pl
from jax.experimental.pallas import tpu as pltpu
from jax.sharding import PartitionSpec as P

MESH = pl.DeviceIdType.MESH
BF = jnp.bfloat16
F32 = jnp.float32

D = 1216
HEADS = 19
HD = 64
TOK = 128
TEXT = 256
BLK = 16
TEXT_COLS = 152
SPARE = 4
ROWS = BLK * TOK
SPARE_ROWS = SPARE * TOK
W_ROWS = 304
SPARE_DEVICES = 4
SPARE_HEADS = 3
QT = 512


def low_half(rows):
    return lax.broadcasted_iota(jnp.int32, (rows, 128), 1) < HD


def swap_halves(value):
    return pltpu.roll(value, HD, axis=1)


def layer_norm(values):
    center = values - jnp.mean(values, axis=-1, keepdims=True)
    return center * lax.rsqrt(jnp.mean(center * center, axis=-1, keepdims=True) + 1e-06)


def pack_heads(source, mains, spares):
    low = low_half(TOK)

    def tile(index):
        return source[:, 128 * index : 128 * index + 128].astype(F32)

    for head in range(HEADS):
        half = head // 2
        if head % 2 == 0:
            packed = jnp.where(low, tile(half), tile(9 + half))
        else:
            packed = swap_halves(jnp.where(low, tile(10 + half), tile(half)))
        if head < BLK:
            mains[head] = packed.astype(BF)
        else:
            spares[head - BLK] = packed.astype(BF)


def kernel(
    sections,
    patch_ref,
    step_ref,
    states_hbm,
    weight_hbm,
    text_weight_ref,
    text_hbm,
    stale_hbm,
    mod_hbm,
    query_gain_ref,
    key_gain_ref,
    text_gain_ref,
    out_hbm,
    fresh_hbm,
    states_v,
    weight_v,
    text_v,
    stale_v,
    mod_v,
    entries_v,
    proj_v,
    fresh_v,
    main_send,
    kv,
    spare_send,
    q_send,
    q_recv,
    q_spare,
    q_all,
    state_recv,
    acc,
    text_send,
    text_recv,
    gate_v,
    out_send,
    load_sem,
    weight_sem,
    main_ssem,
    main_rsem,
    spare_ssem,
    spare_rsem,
    pass_ssem,
    pass_rsem,
    q_ssem,
    q_rsem,
    q_ssem2,
    q_rsem2,
    state_ssem,
    state_rsem,
    state_ssem2,
    state_rsem2,
    text_ssem,
    text_rsem,
    out_ssem,
    out_rsem,
    fresh_sem,
):
    sec = lax.axis_index("section")
    me = lax.axis_index("blk")
    after = lax.rem(sec + 1, sections)
    before = lax.rem(sec + sections - 1, sections)

    load_stale = pltpu.make_async_copy(stale_hbm, stale_v, load_sem.at[0])
    load_states = pltpu.make_async_copy(states_hbm, states_v, load_sem.at[1])
    load_text = pltpu.make_async_copy(text_hbm, text_v, load_sem.at[2])
    load_mod = pltpu.make_async_copy(mod_hbm, mod_v, load_sem.at[3])
    load_stale.start()
    load_states.start()
    load_mod.start()
    load_text.start()
    loads = []
    for part in range(D // W_ROWS):
        rows = pl.ds(part * W_ROWS, W_ROWS)
        loads.append(
            pltpu.make_async_copy(weight_hbm.at[rows], weight_v.at[rows], weight_sem.at[part])
        )
        loads[-1].start()

    barrier = pltpu.get_barrier_semaphore()

    @pl.loop(1, BLK)
    def _(step):
        pl.semaphore_signal(
            barrier, inc=1, device_id=(sec, lax.rem(me + step, BLK)), device_id_type=MESH
        )

    @pl.loop(0, BLK)
    def _(step):
        pl.semaphore_signal(
            barrier, inc=1, device_id=(before, lax.rem(me + step, BLK)), device_id_type=MESH
        )

    core = lax.rem(me, 2)
    chip = me // 2
    sibling = me + 1 - 2 * core
    spare_index = lax.rem(chip, 4)
    has_spare = spare_index < SPARE_HEADS
    first_block = SPARE * (2 * (me // 8) + core)

    def spare_device(index, part):
        return 8 * (part // 2) + 2 * index + lax.rem(part, 2)

    def peer(step):
        ring = step // 4
        up = jnp.where(ring == 0, 2, jnp.where(ring == 1, 1, jnp.where(ring == 2, 3, 0)))
        rest = lax.rem(step, 4)
        to_x = lax.rem(me // 8 + 1 - rest // 2, 2)
        to_y = lax.rem(chip + up, 4)
        to_core = lax.rem(core + 1 - lax.rem(rest, 2), 2)
        return 8 * to_x + 2 * to_y + to_core

    def remote(source, target, send, recv, to, section=None):
        return pltpu.make_async_remote_copy(
            src_ref=source,
            dst_ref=target,
            send_sem=send,
            recv_sem=recv,
            device_id=(sec if section is None else section, to),
            device_id_type=MESH,
        )

    def arrived(ref, sem):
        pltpu.make_async_copy(ref, ref, sem).wait()

    def send_main(kind):
        @pl.loop(0, BLK - 1)
        def _(step):
            to = peer(step)
            remote(
                main_send.at[kind, to],
                kv.at[0, kind, me],
                main_ssem.at[kind],
                main_rsem.at[kind],
                to,
            ).start()

        pltpu.make_async_copy(
            main_send.at[kind, me], kv.at[0, kind, me], main_rsem.at[kind]
        ).start()

    def spare_copy(kind, to_chip):
        return remote(
            spare_send.at[kind, lax.rem(to_chip, 4)],
            kv.at[1, kind, 8 * core + chip],
            spare_ssem.at[kind, to_chip],
            spare_rsem.at[kind],
            2 * to_chip + core,
        )

    def send_spare(kind):
        @pl.loop(0, BLK // 2)
        def _(step):
            to_chip = peer(2 * step) // 2

            @pl.when(jnp.logical_and(to_chip != chip, lax.rem(to_chip, 4) < SPARE_HEADS))
            def _():
                spare_copy(kind, to_chip).start()

        @pl.when(has_spare)
        def _():
            pltpu.make_async_copy(
                spare_send.at[kind, spare_index],
                kv.at[1, kind, 8 * core + chip],
                spare_rsem.at[kind],
            ).start()

    def pass_copy(kind):
        block = kv.at[1, kind, pl.ds(8 * core, 8)]
        return remote(block, block, pass_ssem.at[kind], pass_rsem.at[kind], sibling)

    def pass_spare(kind):
        @pl.when(has_spare)
        def _():
            arrived(kv.at[1, kind, pl.ds(8 * core, 8)], spare_rsem.at[kind])
            pass_copy(kind).start()

    load_stale.wait()
    first_worked = patch_ref[0] == 0
    for index in range(HEADS):
        cols = slice(128 * index, 128 * index + 128)
        entries_v[:, cols] = jnp.where(first_worked, stale_v[1, :, cols], stale_v[0, :, cols])
    pack_heads(entries_v, main_send.at[0], spare_send.at[0])
    pl.semaphore_wait(barrier, 2 * BLK - 1)
    send_main(0)

    load_text.wait()
    load_mod.wait()
    row = step_ref[0]
    text_normed = (
        layer_norm(text_v[...].astype(F32).T) * (1.0 + mod_v[row, 4]) + mod_v[row, 3]
    ).astype(BF)
    text_part = lax.dot_general(
        text_weight_ref[...],
        text_normed,
        (((1,), (1,)), ((), ())),
        preferred_element_type=F32,
    )
    for unit in range(TEXT_COLS // 8):
        eight = text_part[8 * unit : 8 * unit + 8]
        text_send[unit] = jnp.concatenate([eight[:, :128], eight[:, 128:]], axis=0).astype(BF)

    second_half = me // 8
    half_units = TEXT_COLS // 8

    def text_pieces(place):
        pieces = []
        unit = half_units * place
        while unit < half_units * (place + 1):
            head = unit // 8
            end = min(8 * head + 8, half_units * (place + 1))
            pieces.append((unit - half_units * place, end - unit, head, unit % 8))
            unit = end
        return pieces

    def text_copies(act, act_local):
        for place in range(8):

            @pl.when(lax.rem(me, 8) == place)
            def _():
                for number, (row, units, head, to_row) in enumerate(text_pieces(place)):
                    spare = head >= BLK
                    source = text_send.at[pl.ds(row, units)]
                    target = text_recv.at[int(spare), pl.ds(8 * second_half + to_row, units)]

                    @pl.loop(0, SPARE_DEVICES if spare else 1)
                    def _(step):
                        to = spare_device(head - BLK, step) if spare else jnp.int32(head)

                        @pl.when(to != me)
                        def _():
                            act(
                                remote(
                                    source,
                                    target,
                                    text_ssem.at[number, step],
                                    text_rsem.at[int(spare)],
                                    to,
                                )
                            )

                        @pl.when(to == me)
                        def _():
                            act_local(source, target, text_rsem.at[int(spare)])

    text_copies(
        lambda copy: copy.start(),
        lambda source, target, sem: pltpu.make_async_copy(source, target, sem).start(),
    )

    slot_there = lax.rem(me, SPARE)

    def spare_target(index):
        return spare_device(index, me // SPARE)

    def query_copy(index):
        return remote(
            q_send.at[BLK + index],
            q_spare.at[slot_there],
            q_ssem2.at[index],
            q_rsem2.at[slot_there],
            spare_target(index),
        )

    def state_rows(head):
        return states_v.at[pl.ds(pl.multiple_of(HD * head, HD), HD)]

    def state_copy(index):
        return remote(
            state_rows(BLK + index),
            state_recv.at[BLK + slot_there],
            state_ssem2.at[index],
            state_rsem2.at[slot_there],
            spare_target(index),
        )

    load_states.wait()
    normed = (
        layer_norm(states_v[...].astype(F32).T) * (1.0 + mod_v[row, 1]) + mod_v[row, 0]
    ).astype(BF)
    for load in loads:
        load.wait()

    block_ones = (
        (lax.broadcasted_iota(jnp.int32, (128, 128), 0) < HD)
        == (lax.broadcasted_iota(jnp.int32, (128, 128), 1) < HD)
    ).astype(BF)
    query_gain = query_gain_ref[...]
    key_gain = key_gain_ref[...]

    def project(first, last):
        proj_v[:, first:last] = jnp.dot(
            normed, weight_v[:, first:last], preferred_element_type=F32
        )

    def normed_tile(index):
        value = proj_v[:, 128 * index : 128 * index + 128]
        square = value * value
        high = square.astype(BF)
        low = (square - high.astype(F32)).astype(BF)
        mean = (
            jnp.dot(high, block_ones, preferred_element_type=F32)
            + jnp.dot(low, block_ones, preferred_element_type=F32)
        ) * (1.0 / HD)
        gain = jnp.concatenate(
            [
                query_gain if index < 10 else key_gain,
                query_gain if index < 9 else key_gain,
            ],
            axis=1,
        )
        return value * lax.rsqrt(mean + 1e-06) * gain

    low64 = low_half(HD)
    project(0, 1280)
    for index in range(10):
        value = normed_tile(index)
        if index == 9:
            proj_v[:, 128 * index : 128 * index + 128] = value
        top, bottom = value[:HD], value[HD:]
        even = jnp.where(low64, top, swap_halves(bottom))
        q_send[2 * index] = (even.astype(BF).astype(F32) * 0.125).astype(BF)
        if index < 9:
            odd = jnp.where(low64, swap_halves(top), bottom)
            q_send[2 * index + 1] = (odd.astype(BF).astype(F32) * 0.125).astype(BF)

    @pl.loop(0, BLK - 1)
    def _(step):
        to = peer(step)
        remote(q_send.at[to], q_recv.at[me], q_ssem, q_rsem, to).start()

    pltpu.make_async_copy(q_send.at[me], q_recv.at[me], q_rsem).start()

    for index in range(SPARE_HEADS):

        @pl.when(spare_target(index) != me)
        def _():
            query_copy(index).start()

        @pl.when(spare_target(index) == me)
        def _():
            pltpu.make_async_copy(
                q_send.at[BLK + index], q_spare.at[slot_there], q_rsem2.at[slot_there]
            ).start()

    @pl.loop(0, BLK - 1)
    def _(step):
        to = peer(step)
        remote(state_rows(to), state_recv.at[me], state_ssem, state_rsem, to).start()

    pltpu.make_async_copy(state_rows(me), state_recv.at[me], state_rsem).start()
    for index in range(SPARE_HEADS):

        @pl.when(spare_target(index) != me)
        def _():
            state_copy(index).start()

        @pl.when(spare_target(index) == me)
        def _():
            pltpu.make_async_copy(
                state_rows(BLK + index), state_recv.at[BLK + slot_there], state_rsem2.at[slot_there]
            ).start()

    project(1280, 2432)
    project(2432, 3648)
    low = low_half(TOK)

    def swapped_tile(index):
        if index == 9 or index >= 19:
            return swap_halves(proj_v[:, 128 * index : 128 * index + 128])
        return swap_halves(normed_tile(index))

    left = swapped_tile(9)
    for index in range(HEADS):
        right = swapped_tile(10 + index)
        fresh_v[:, 128 * index : 128 * index + 128] = jnp.where(low, left, right).astype(BF)
        left = right
    fresh_copy = pltpu.make_async_copy(fresh_v, fresh_hbm, fresh_sem)
    fresh_copy.start()
    pack_heads(fresh_v, main_send.at[1], spare_send.at[1])
    send_main(1)

    send_spare(0)
    send_spare(1)

    one = jnp.ones((1, 128), F32)
    low1 = low_half(1)
    gate_pad = jnp.concatenate([mod_v[row, 2], jnp.zeros((1, 64), F32)], axis=1)
    for head in range(HEADS):
        gate = gate_pad[:, 128 * (head // 2) : 128 * (head // 2) + 128]
        if head % 2 == 0:
            gate = swap_halves(jnp.broadcast_to(gate, (8, 128)))[0:1]
        gate_v[head : head + 1, :] = jnp.where(low1, one, gate)

    arrived(q_recv, q_rsem)

    def spread_queries(packed, row):
        value = packed.astype(F32)
        zero = jnp.zeros_like(value)
        q_all[pl.ds(row, HD)] = jnp.where(low64, value, zero).astype(BF)
        q_all[pl.ds(row + HD, HD)] = jnp.where(low64, swap_halves(value), zero).astype(BF)

    @pl.loop(0, BLK)
    def _(step):
        spread_queries(q_recv[step], pl.multiple_of(step * TOK, TOK))

    @pl.when(has_spare)
    def _():
        for slot in range(SPARE):
            arrived(q_spare.at[slot], q_rsem2.at[slot])
            spread_queries(q_spare[slot], ROWS + slot * TOK)

    def with_ones(entries):
        return jnp.where(
            low_half(entries.shape[0]), jnp.ones(entries.shape, F32), entries.astype(F32)
        ).astype(BF)

    def attend(rows, entries, values):
        scores = lax.dot_general(
            q_all[rows], entries, (((1,), (1,)), ((), ())), preferred_element_type=F32
        )
        powers = jnp.exp(scores).astype(BF)
        return jnp.dot(powers, values, preferred_element_type=F32)

    low256 = low_half(TEXT)
    text_gain = jnp.concatenate([text_gain_ref[...], jnp.ones((1, HD), F32)], axis=1)

    def take_text(which):
        arrived(text_recv.at[which], text_rsem.at[which])
        tiles = text_recv[which].astype(F32)
        halves = [tiles[:, 8 * half : 8 * half + 8].reshape(128, 128) for half in range(2)]
        value = jnp.concatenate([halves[0].T, halves[1].T], axis=0)
        square = jnp.where(low256, value * value, 0.0)
        mean = jnp.sum(square, axis=1, keepdims=True) * (1.0 / HD)
        scaled = value * lax.rsqrt(mean + 1e-06) * text_gain
        entries = jnp.where(low256, scaled, value).astype(BF)
        kv[which, 0, BLK] = entries[:TOK]
        kv[which, 1, BLK] = entries[TOK:]

    take_text(0)

    @pl.when(has_spare)
    def _():
        take_text(1)

    acc[...] = jnp.zeros_like(acc)
    arrived(kv.at[0, 0, pl.ds(0, BLK)], main_rsem.at[0])

    tiles = ROWS // QT
    per_tile = QT // TOK

    def result_copy(slot):
        main = slot < BLK
        head = jnp.where(main, me, BLK + spare_index)
        target = out_hbm.at[pl.ds(pl.multiple_of(HD * head, HD), HD)]
        block = jnp.where(main, slot, first_block + slot - BLK)
        return remote(out_send.at[slot], target, out_ssem.at[slot], out_rsem, block, after)

    @pl.loop(0, 2 * tiles + 2)
    def _(item):
        @pl.when(item == tiles)
        def _():
            arrived(kv.at[0, 1, pl.ds(0, BLK)], main_rsem.at[1])
            arrived(state_recv.at[pl.ds(0, BLK)], state_rsem)

        @pl.when(item == tiles + 1)
        def _():
            pass_spare(0)

        @pl.when(item == 2 * tiles - 1)
        def _():
            pass_spare(1)

        main = item < 2 * tiles
        kind = jnp.where(main, item // tiles, item - 2 * tiles)
        which = jnp.where(main, 0, 1)
        step = jnp.where(main, lax.rem(me + item, tiles), tiles)

        @pl.when(jnp.logical_and(has_spare, jnp.logical_not(main)))
        def _():
            arrived(kv.at[1, kind, pl.ds(8 * (1 - core), 8)], pass_rsem.at[kind])

        @pl.when(jnp.logical_or(has_spare, main))
        def _():
            rows = pl.ds(pl.multiple_of(step * QT, QT), QT)
            entries = kv[which, kind].reshape((BLK + 1) * TOK, 128)
            acc[rows] += attend(rows, entries, with_ones(entries))

        @pl.when(jnp.logical_and(has_spare, item == 2 * tiles + 1))
        def _():
            for slot in range(SPARE):
                arrived(state_recv.at[BLK + slot], state_rsem2.at[slot])

        @pl.when(jnp.logical_and(kind == 1, jnp.logical_or(has_spare, main)))
        def _():
            gate = gate_v[pl.ds(jnp.where(main, me, BLK + spare_index), 1), :]

            @pl.loop(0, per_tile)
            def _(turn):
                part = lax.rem(turn + me // per_tile, per_tile)
                slot = step * per_tile + part
                value = acc[pl.ds(pl.multiple_of(slot * TOK, TOK), TOK)] * gate
                turned = value.T
                out_send[slot] = (
                    state_recv[slot].astype(F32) + turned[HD:] / turned[:HD]
                ).astype(BF)
                result_copy(slot).start()

    arrived(out_hbm, out_rsem)

    fresh_copy.wait()
    for kind in range(2):
        arrived(main_send.at[kind, pl.ds(0, BLK - 1)], main_ssem.at[kind])

        @pl.loop(0, BLK // 2)
        def _(to_chip):
            @pl.when(jnp.logical_and(to_chip != chip, lax.rem(to_chip, 4) < SPARE_HEADS))
            def _():
                spare_copy(kind, to_chip).wait_send()

    arrived(q_send.at[pl.ds(0, BLK - 1)], q_ssem)
    arrived(state_recv.at[pl.ds(0, BLK - 1)], state_ssem)
    for index in range(SPARE_HEADS):

        @pl.when(spare_target(index) != me)
        def _():
            query_copy(index).wait_send()
            state_copy(index).wait_send()

    text_copies(lambda copy: copy.wait_send(), lambda *_: None)

    @pl.loop(0, BLK)
    def _(slot):
        result_copy(slot).wait_send()

    @pl.when(has_spare)
    def _():
        for slot in range(SPARE):
            result_copy(BLK + slot).wait_send()
        for kind in range(2):
            pass_copy(kind).wait_send()


def write_results(raw_states, raw_fresh, states_out, fresh_out, states_v, fresh_v, sems):
    loads = (
        pltpu.make_async_copy(raw_fresh, fresh_v, sems.at[0]),
        pltpu.make_async_copy(raw_states, states_v, sems.at[1]),
    )
    stores = (
        pltpu.make_async_copy(fresh_v, fresh_out, sems.at[0]),
        pltpu.make_async_copy(states_v, states_out, sems.at[1]),
    )
    for load in loads:
        load.start()
    for load, store in zip(loads, stores):
        load.wait()
        store.start()
    for store in stores:
        store.wait()


def body(
    sections,
    states,
    image_weight,
    text_weight,
    text_states,
    stale_cache,
    modulation,
    query_gain,
    key_gain,
    text_gain,
    timestep,
    layer_patch_index,
):
    vmem = pl.BlockSpec(memory_space=pltpu.VMEM)
    anywhere = pl.BlockSpec(memory_space=pl.ANY)
    dma = pltpu.SemaphoreType.DMA
    next_states, fresh = pl.pallas_call(
        functools.partial(kernel, sections),
        out_shape=(
            jax.ShapeDtypeStruct((D, TOK), BF),
            jax.ShapeDtypeStruct((TOK, 2 * D), BF),
        ),
        in_specs=[
            pl.BlockSpec(memory_space=pltpu.SMEM),
            pl.BlockSpec(memory_space=pltpu.SMEM),
            anywhere,
            anywhere,
            vmem,
            anywhere,
            anywhere,
            anywhere,
            vmem,
            vmem,
            vmem,
        ],
        out_specs=(anywhere, anywhere),
        scratch_shapes=[
            pltpu.VMEM((D, TOK), BF),
            pltpu.VMEM((D, 3 * D), BF),
            pltpu.VMEM((D, TEXT), BF),
            pltpu.VMEM((2, TOK, 2 * D), BF),
            pltpu.VMEM((modulation.shape[0], 5, 1, D), F32),
            pltpu.VMEM((TOK, 2 * D), BF),
            pltpu.VMEM((TOK, 3 * D + 64), F32),
            pltpu.VMEM((TOK, 2 * D), BF),
            pltpu.VMEM((2, BLK, TOK, 128), BF),
            pltpu.VMEM((2, 2, BLK + 1, TOK, 128), BF),
            pltpu.VMEM((2, SPARE_HEADS, TOK, 128), BF),
            pltpu.VMEM((HEADS, HD, 128), BF),
            pltpu.VMEM((BLK, HD, 128), BF),
            pltpu.VMEM((SPARE, HD, 128), BF),
            pltpu.VMEM((ROWS + SPARE_ROWS, 128), BF),
            pltpu.VMEM((BLK + SPARE, HD, 128), BF),
            pltpu.VMEM((ROWS + SPARE_ROWS, 128), F32),
            pltpu.VMEM((TEXT_COLS // 8, 16, 128), BF),
            pltpu.VMEM((2, 16, 16, 128), BF),
            pltpu.VMEM((24, 128), F32),
            pltpu.VMEM((BLK + SPARE, HD, 128), BF),
            dma((4,)),
            dma((D // W_ROWS,)),
            dma((2,)),
            dma((2,)),
            dma((2, BLK // 2)),
            dma((2,)),
            dma((2,)),
            dma((2,)),
            dma,
            dma,
            dma((SPARE_HEADS,)),
            dma((SPARE,)),
            dma,
            dma,
            dma((SPARE_HEADS,)),
            dma((SPARE,)),
            dma((4, SPARE_DEVICES)),
            dma((2,)),
            dma((BLK + SPARE,)),
            dma,
            dma,
        ],
        compiler_params=pltpu.CompilerParams(
            collective_id=0, has_side_effects=True, vmem_limit_bytes=56 * 1024 * 1024
        ),
    )(
        layer_patch_index,
        timestep,
        jnp.swapaxes(states[0], 0, 1),
        image_weight[0],
        jnp.swapaxes(text_weight[0], 0, 1),
        jnp.swapaxes(text_states[0], 0, 1),
        stale_cache[0],
        jnp.swapaxes(modulation, 1, 2),
        query_gain,
        key_gain,
        text_gain,
    )
    next_states, fresh = pl.pallas_call(
        write_results,
        out_shape=(
            jax.ShapeDtypeStruct((D, TOK), BF),
            jax.ShapeDtypeStruct((TOK, 2 * D), BF),
        ),
        in_specs=[anywhere, anywhere],
        out_specs=(anywhere, anywhere),
        scratch_shapes=[pltpu.VMEM((D, TOK), BF), pltpu.VMEM((TOK, 2 * D), BF), dma((2,))],
        compiler_params=pltpu.CompilerParams(vmem_limit_bytes=60 * 1024 * 1024),
    )(next_states, fresh)
    return (jnp.swapaxes(next_states, 0, 1)[None], fresh[None])


def solution(mesh):
    in_specs = (
        P("section", "blk", None),
        P("section", None, None),
        P("section", None, "blk"),
        P("section", None, None),
        P("section", None, "blk", None),
        P(None, "section", None, None),
        P("section", None),
        P("section", None),
        P("section", None),
        P("section"),
        P("section"),
    )
    out_specs = (P("section", "blk", None), P("section", "blk", None))
    return jax.shard_map(
        functools.partial(body, mesh.shape["section"]),
        mesh=mesh,
        in_specs=in_specs,
        out_specs=out_specs,
        check_vma=False,
    )
```
